32 devices in a mesh: parts: 2 (over y), beam: 8 (over z, x), head: 2 (over core).
Axes of the slice: x: 2, y: 2, z: 4, core: 2. Of those that a mesh axis runs over, the one named last changes fastest.
Arguments:
- states: float32 [32, 128, 4096], P(('parts', 'beam'), None, 'head'), parts along dimension 0, may hold values from -6 to 6
- decay_rates: float32 [32], P('head'), may hold values from 0.05 to 2
- queries: bfloat16 [2, 32, 4096], P(None, ('parts', 'beam'), 'head'), parts along dimension 1, may hold values from -0.59765625 to 0.59765625
- key_vectors: bfloat16 [2, 32, 4096], P(None, ('parts', 'beam'), 'head'), parts along dimension 1, may hold values from -6 to 6
- values: bfloat16 [2, 32, 4096], P(None, ('parts', 'beam'), 'head'), parts along dimension 1, may hold values from -6 to 6
- gate_logits: bfloat16 [2, 32, 4096], P(None, ('parts', 'beam'), 'head'), parts along dimension 1, may hold values from -6 to 6
- parents: int32 [2, 32], P(None, 'parts'), parts along dimension 1, may hold values from 0 to 15, as said below
- out_weight: bfloat16 [4096, 6144], P('head', 'beam'), may hold values from -0.09375 to 0.09375
Outputs:
- projected: bfloat16 [2, 32, 6144], P(None, ('parts', 'head'), 'beam'), parts along dimension 1
- final_states: float32 [32, 128, 4096], P(('parts', 'beam'), None, 'head'), parts along dimension 0
The draws below stay inside these ranges and needn't reach their ends.
There are 2 independent parts, one for each index of `parts`. The reference program is written for one: setup_inputs(seed, part) draws one part's arguments, and reference() takes and returns one part's arrays. A program takes and returns all parts, laid end to end along the dimension named above; an argument that names none is the same for every part. Nothing has to cross between parts.
Inputs may be any that keep to these rules, and one draw needn't show every extreme that they name: Beam j of request r sits in slot j * 2 + r; a parent is a slot of the same request (parents[t, c] % 2 == c % 2); beam 0 of every request is the child of beam 0, and the last slot is the child of itself at each step.
All inputs are finite; a program needn't handle non-finite values.
Results may differ from the reference program's by a relative error of at most 0.0049.
Values may be sent and summed in bfloat16 or wider, within the bound.
No kernel may reach another device: no remote copies, remote signals or barrier semaphores. Data moves between devices by JAX's collectives and lax.ppermute only.
A program may use at most 64 MiB of HBM per device.

```python
import math
import jax
import jax.numpy as jnp
from jax import lax

D = 6144
HEADS = 32
HEAD_DIM = 128
WIDTH = 8
STEPS = 2
BEAMS = 16
REQUESTS = 2


def draw_parents(key, part):
    key = jax.random.fold_in(key, 11)
    slots = jnp.arange(BEAMS, dtype=jnp.int32)
    picks = jax.random.randint(key, (3, STEPS, BEAMS), 0, WIDTH)
    chosen = jnp.min(picks, axis=0)
    child_beam = slots // REQUESTS
    chosen = jnp.where(child_beam[None, :] == 0, 0, chosen)
    chosen = jnp.where(slots[None, :] == BEAMS - 1, WIDTH - 1, chosen)
    return (chosen * REQUESTS + (slots % REQUESTS)[None, :]).astype(jnp.int32)


def level_of(stream_key, extent, cuts, low, largest):
    loudness, own = 1.0, jax.random.fold_in(stream_key, 6)
    for axis_at, blocks in cuts:
        draws = jnp.exp(jax.random.uniform(jax.random.fold_in(own, axis_at), (blocks,), jnp.float32, low / len(cuts), largest / len(cuts)))
        loudness = loudness * jnp.repeat(draws, extent[axis_at] // blocks).reshape([-1 if axis == axis_at else 1 for axis in range(len(extent))])
    return loudness


def normal_values(rng, dims, spread, most, pieces=(), kind=jnp.bfloat16):
    drawn = spread * jax.random.normal(rng, dims, jnp.float32)
    if pieces:
        drawn = drawn * level_of(rng, dims, pieces, -0.22, 0.18)
    return jnp.clip(drawn, -most, most).astype(kind)


def setup_inputs(seed: int = 0, part: int = 0) -> dict:
    key_list = jax.random.split(jax.random.key(seed), 9)
    part_keys = jax.random.split(jax.random.fold_in(key_list[8], part), 9)
    states = normal_values(part_keys[0], (BEAMS, HEAD_DIM, HEADS * HEAD_DIM), 1.0, 6.0, ((0, 8), (2, 2)), jnp.float32)
    decay_rates = jnp.clip(jnp.exp(math.log(2.0) - 3.6888794 * jax.random.uniform(key_list[1], (HEADS,), jnp.float32) ** level_of(key_list[1], (HEADS,), ((0, 2),), -0.2, 0.2)), 0.05, 2.0)
    queries = normal_values(part_keys[2], (STEPS, BEAMS, HEADS * HEAD_DIM), 0.0884, 0.59765625, ((1, 8), (2, 2)))
    key_vectors = normal_values(part_keys[3], (STEPS, BEAMS, HEADS * HEAD_DIM), 1.0, 6.0, ((1, 8), (2, 2)))
    values = normal_values(part_keys[4], (STEPS, BEAMS, HEADS * HEAD_DIM), 1.0, 6.0, ((1, 8), (2, 2)))
    gate_logits = normal_values(part_keys[5], (STEPS, BEAMS, HEADS * HEAD_DIM), 1.0, 6.0, ((1, 8), (2, 2)))
    parents = draw_parents(jax.random.fold_in(jax.random.fold_in(key_list[8], part), 71), part)
    out_weight = normal_values(key_list[7], (HEADS * HEAD_DIM, D), (HEADS * HEAD_DIM) ** -0.5, 0.09375, ((0, 2), (1, 8)))
    return dict(states=states, decay_rates=decay_rates, queries=queries, key_vectors=key_vectors, values=values, gate_logits=gate_logits, parents=parents, out_weight=out_weight)


def step_state(state, decay, query, key_row, value_row):
    query_f = query.astype(jnp.float32).reshape(HEADS, HEAD_DIM)
    key_f = key_row.astype(jnp.float32).reshape(HEADS, HEAD_DIM)
    value_f = value_row.astype(jnp.float32).reshape(HEADS, HEAD_DIM)
    updated = decay[None, :, None] * state + jnp.einsum('hi,hj->ihj', key_f, value_f)
    readout = jnp.einsum('hi,ihj->hj', query_f, updated, precision=lax.Precision.HIGHEST)
    return updated, readout.reshape(HEADS * HEAD_DIM)


def reference(states, decay_rates, queries, key_vectors, values, gate_logits, parents, out_weight):
    decay = jnp.exp(-decay_rates)
    grid = states.reshape(BEAMS, HEAD_DIM, HEADS, HEAD_DIM)

    def per_slot(child):
        middle = parents[1, child]
        root = parents[0, middle]
        own = parents[0, child]
        first_state, first_readout = step_state(grid[own], decay, queries[0, child], key_vectors[0, child], values[0, child])
        middle_state, unused = step_state(grid[root], decay, queries[0, middle], key_vectors[0, middle], values[0, middle])
        second_state, second_readout = step_state(middle_state, decay, queries[1, child], key_vectors[1, child], values[1, child])
        return second_state, first_readout, second_readout

    final, first, second = lax.map(per_slot, jnp.arange(BEAMS, dtype=jnp.int32))
    readouts = jnp.stack([first, second])
    attn = (jax.nn.sigmoid(gate_logits.astype(jnp.float32)) * readouts).astype(jnp.bfloat16)
    projected = jnp.einsum('tbc,cd->tbd', attn.astype(jnp.float32), out_weight.astype(jnp.float32))
    return projected.astype(jnp.bfloat16), final.reshape(BEAMS, HEAD_DIM, HEADS * HEAD_DIM)
```

```python
import functools

import jax
import jax.numpy as jnp
from jax import lax
from jax.experimental import pallas as pl
from jax.experimental.pallas import tpu as pltpu
from jax.sharding import PartitionSpec as P

F32, BF16 = jnp.float32, jnp.bfloat16
VMEM = pl.BlockSpec(memory_space=pltpu.VMEM)
SMEM = pl.BlockSpec(memory_space=pltpu.SMEM)
ANY = pl.BlockSpec(memory_space=pl.ANY)
STEPS, ARRAYS = 2, 4
Q, K, V, G = range(ARRAYS)
EXTRA = 16


def params(limit=48):
    return pltpu.CompilerParams(vmem_limit_bytes=limit << 20)


def cost(flops, moved):
    return pl.CostEstimate(flops=flops, bytes_accessed=moved, transcendentals=0)


def row_of(head, array, step):
    return head * ARRAYS * STEPS + array * STEPS + step


def pack_kernel(n, st, q, k, v, g, *rest):
    outs, rows = rest[:n], rest[n]
    slots, dim, columns = st.shape
    heads = columns // dim // n
    me = lax.axis_index("beam")
    for a, ref in enumerate((q, k, v, g)):
        whole = ref[...].astype(F32)
        for t in range(STEPS):
            for j in range(slots):
                rows[j, a * STEPS + t : a * STEPS + t + 1, :] = whole[t, j : j + 1]
    for x in range(n):
        first = (me ^ x) * heads
        for j in range(slots):
            extra = []
            for i in range(heads):
                at = pl.ds(pl.multiple_of((first + i) * dim, dim), dim)
                outs[x][j, i * dim : (i + 1) * dim, :] = st[j, :, at].astype(BF16)
                extra.append(rows[j, :, at])
            outs[x][j, heads * dim :, :] = jnp.concatenate(extra, 0).astype(BF16)


def pick_kernel(n, parents, *rest):
    ins, outs, (buf, sem_in, sem_out) = rest[:n], rest[n : 2 * n], rest[2 * n :]
    slots, rows, _ = ins[0].shape
    depth = rows - EXTRA
    me = lax.axis_index("beam")
    copies = []
    for x in range(n):
        at = pl.multiple_of((me ^ x) * slots, slots)
        copies.append(pltpu.make_async_copy(ins[x], buf.at[pl.ds(at, slots)], sem_in.at[x]))
        copies[-1].start()
    for c in copies:
        c.wait()
    copies = []
    for x in range(n):
        for j in range(slots):
            middle = parents[1, (me ^ x) * slots + j]
            root = parents[0, middle]
            copies.append(
                pltpu.make_async_copy(
                    buf.at[root, pl.ds(0, depth)], outs[x].at[j, pl.ds(0, depth)], sem_out.at[x, j, 0]
                )
            )
            copies.append(
                pltpu.make_async_copy(
                    buf.at[middle, pl.ds(depth, EXTRA)], outs[x].at[j, pl.ds(depth, EXTRA)], sem_out.at[x, j, 1]
                )
            )
            copies[-2].start()
            copies[-1].start()
    for c in copies:
        c.wait()


def readout_kernel(n, parents, decay, *rest):
    ins, out, vectors = rest[:n], rest[n], rest[n + 1]
    slots, rows, dim = ins[0].shape
    heads = (rows - EXTRA) // dim
    total = n * slots
    me = lax.axis_index("beam")
    for x in range(n):
        for j in range(slots):
            at = pl.multiple_of(((me ^ x) * slots + j) * EXTRA, EXTRA)
            vectors[pl.ds(at, EXTRA), :] = ins[x][j, heads * dim :, :].astype(F32)
    line = lax.broadcasted_iota(jnp.int32, (STEPS * total, dim), 0)
    mid_line = lax.broadcasted_iota(jnp.int32, (total, total), 0)
    source = jnp.zeros((STEPS * total, dim), jnp.int32)
    chosen = jnp.zeros((total, total), jnp.int32)
    for c in range(total):
        middle = parents[1, c]
        source = jnp.where(line == c, parents[0, c], source)
        source = jnp.where(line == total + c, parents[0, middle], source)
        chosen = jnp.where(mid_line == c, middle, chosen)
    pick = (chosen == lax.broadcasted_iota(jnp.int32, (total, total), 1)).astype(BF16)
    for i in range(heads):
        d = decay[me * heads + i]

        def get(array, step):
            return vectors[pl.ds(row_of(i, array, step), total, stride=EXTRA), :]

        q1, q2, k1, k2 = get(Q, 0), get(Q, 1), get(K, 0), get(K, 1)
        v1, v2 = get(V, 0), get(V, 1)
        queries = jnp.concatenate([q1, q2], 0)
        acc = jnp.zeros((STEPS * total, dim), F32)
        for x in range(n):
            for j in range(slots):
                slot = (me ^ x) * slots + j
                mine = jnp.where(source == slot, queries, 0.0).astype(BF16)
                acc += jnp.dot(mine, ins[x][j, i * dim : (i + 1) * dim, :], preferred_element_type=F32)
        k1m = jnp.dot(pick, k1.astype(BF16), preferred_element_type=F32)
        v1m = jnp.dot(pick, v1.astype(BF16), preferred_element_type=F32)
        r1 = d * acc[:total] + jnp.sum(q1 * k1, -1, keepdims=True) * v1
        r2 = d * (d * acc[total:] + jnp.sum(q2 * k1m, -1, keepdims=True) * v1m)
        r2 = r2 + jnp.sum(q2 * k2, -1, keepdims=True) * v2
        lanes = slice(i * dim, (i + 1) * dim)
        out[:total, lanes] = (jax.nn.sigmoid(get(G, 0)) * r1).astype(BF16)
        out[total:, lanes] = (jax.nn.sigmoid(get(G, 1)) * r2).astype(BF16)


def project_kernel(order, head_count, mine, theirs, weight, keep, send, terms):
    me, head = lax.axis_index("beam"), lax.axis_index("head")
    half, lines, depth = mine.shape
    acc = None
    for at, x in enumerate(order):
        rows = pl.ds(pl.multiple_of((me ^ x) * depth, depth), depth)
        lhs = mine[at] if at < half else theirs[at - half]
        term = jnp.dot(lhs, weight[rows, :], preferred_element_type=F32)
        acc = term if acc is None else acc + term
    terms[...] = acc
    part = lines // STEPS // head_count
    for t in range(STEPS):
        own = pl.multiple_of(t * part * head_count + head * part, part)
        other = pl.multiple_of(t * part * head_count + (1 - head) * part, part)
        keep[t] = terms[pl.ds(own, part), :]
        send[t] = terms[pl.ds(other, part), :]


def final_kernel(n, decay, k, v, *rest):
    ins, out, ks, vs = rest[:n], rest[n], rest[n + 1], rest[n + 2]
    slots, rows, dim = ins[0].shape
    heads = (rows - EXTRA) // dim
    me = lax.axis_index("beam")
    ks[...] = k[1].astype(F32)
    vs[...] = v[1].astype(F32)
    line = lax.broadcasted_iota(jnp.int32, (16, dim), 0)
    for x in range(n):
        for j in range(slots):
            extra = ins[x][j, heads * dim :, :].astype(F32)
            for i in range(heads):
                h = (me ^ x) * heads + i
                d = decay[h]
                at = pl.ds(pl.multiple_of(h * dim, dim), dim)
                at_k, at_v = row_of(i, K, 0), row_of(i, V, 0)
                k1, v1 = extra[at_k : at_k + 1], extra[at_v : at_v + 1]
                scaled = d * v1
                high = scaled.astype(BF16).astype(F32)
                low = scaled - high
                lhs = jnp.where(line < 2, k1, jnp.where(line == 2, ks[j : j + 1, at], 0.0))
                rhs = jnp.where(line == 0, high, jnp.where(line == 1, low, vs[j : j + 1, at]))
                outer = lax.dot_general(
                    lhs.astype(BF16), rhs.astype(BF16), (((0,), (0,)), ((), ())), preferred_element_type=F32
                )
                out[j, :, at] = (d * d) * ins[x][j, i * dim : (i + 1) * dim, :].astype(F32) + outer


def fast(n, head_count, states, decay_rates, queries, key_vectors, values, gate_logits, parents, out_weight):
    slots, dim, columns = states.shape
    heads = columns // dim // n
    total = n * slots
    rows = heads * dim + EXTRA
    chunk = jax.ShapeDtypeStruct((slots, rows, dim), BF16)
    decay = jnp.exp(-decay_rates)

    def swap(array, x):
        return lax.ppermute(array, "beam", [(j, j ^ x) for j in range(n)])

    packed = pl.pallas_call(
        functools.partial(pack_kernel, n),
        out_shape=[chunk] * n,
        in_specs=[VMEM] * 5,
        out_specs=[VMEM] * n,
        scratch_shapes=[pltpu.VMEM((slots, ARRAYS * STEPS, columns), F32)],
        compiler_params=params(),
    )(states, queries, key_vectors, values, gate_logits)
    middle = [packed[0]] + [swap(packed[x], x) for x in range(1, n)]
    picked = pl.pallas_call(
        functools.partial(pick_kernel, n),
        out_shape=[chunk] * n,
        in_specs=[SMEM] + [ANY] * n,
        out_specs=[ANY] * n,
        scratch_shapes=[
            pltpu.VMEM((total, rows, dim), BF16),
            pltpu.SemaphoreType.DMA((n,)),
            pltpu.SemaphoreType.DMA((n, slots, 2)),
        ],
        compiler_params=params(),
    )(parents, *middle)
    forked = [picked[0]] + [swap(picked[x], x) for x in range(1, n)]
    attn = pl.pallas_call(
        functools.partial(readout_kernel, n),
        out_shape=jax.ShapeDtypeStruct((STEPS * total, heads * dim), BF16),
        in_specs=[SMEM, SMEM] + [VMEM] * n,
        out_specs=VMEM,
        scratch_shapes=[pltpu.VMEM((total * EXTRA, dim), F32)],
        compiler_params=params(),
    )(parents, decay, *middle)
    have, order, hop = attn[None], [0], n // 2
    while hop:
        got = swap(have, hop)
        order = order + [x ^ hop for x in order]
        if hop > 1:
            have = jnp.concatenate([have, got], 0)
        hop //= 2
    part = total // head_count
    piece = jax.ShapeDtypeStruct((STEPS, part, out_weight.shape[1]), F32)
    keep, send = pl.pallas_call(
        functools.partial(project_kernel, order, head_count),
        out_shape=[piece, piece],
        in_specs=[VMEM] * 3,
        out_specs=[VMEM] * 2,
        scratch_shapes=[pltpu.VMEM((STEPS * total, out_weight.shape[1]), F32)],
        compiler_params=params(),
    )(have, got, out_weight)
    other = lax.ppermute(send, "head", [(0, 1), (1, 0)])
    projected = (keep + other).astype(BF16)
    final = pl.pallas_call(
        functools.partial(final_kernel, n),
        out_shape=jax.ShapeDtypeStruct(states.shape, F32),
        in_specs=[SMEM] + [VMEM] * (n + 2),
        out_specs=VMEM,
        scratch_shapes=[pltpu.VMEM((slots, columns), F32)] * 2,
        compiler_params=params(),
    )(decay, key_vectors, values, *forked)
    return projected, final


def fork(state, parent_list):
    row_state = lax.all_to_all(state, "beam", split_axis=1, concat_axis=0, tiled=True)
    picked = jnp.take(row_state, parent_list, axis=0)
    return lax.all_to_all(picked, "beam", split_axis=0, concat_axis=1, tiled=True)


def general(states, decay_rates, queries, key_vectors, values, gate_logits, parents, out_weight):
    slot_count, head_dim, columns = states.shape
    groups = columns // head_dim
    decay = jnp.exp(-decay_rates)
    current = states
    readouts = []
    for step in range(parents.shape[0]):
        forked = fork(current, parents[step])
        query_f = queries[step].astype(F32).reshape(slot_count, groups, head_dim)
        key_f = key_vectors[step].astype(F32).reshape(slot_count, groups, head_dim)
        value_f = values[step].astype(F32).reshape(slot_count, groups, head_dim)
        grid = forked.reshape(slot_count, head_dim, groups, head_dim)
        updated = decay[None, None, :, None] * grid + jnp.einsum("shi,shj->sihj", key_f, value_f)
        readout = jnp.einsum("shi,sihj->shj", query_f, updated, precision=lax.Precision.HIGHEST)
        current = updated.reshape(slot_count, head_dim, columns)
        readouts.append(readout.reshape(slot_count, columns))
    stacked = jnp.stack(readouts)
    attn = (jax.nn.sigmoid(gate_logits.astype(F32)) * stacked).astype(BF16)
    terms = jnp.einsum(
        "tsc,cd->tsd",
        lax.all_gather(attn, "beam", axis=1, tiled=True),
        out_weight,
        preferred_element_type=F32,
    )
    projected = lax.psum_scatter(terms, "head", scatter_dimension=1, tiled=True).astype(BF16)
    return (projected, current)


def solution(mesh):
    n, head_count = mesh.shape["beam"], mesh.shape["head"]

    def shards(*args):
        columns, dim = args[0].shape[2], args[0].shape[1]
        if n & (n - 1) == 0 and columns // dim == 2 * n and head_count == 2:
            return fast(n, head_count, *args)
        return general(*args)

    in_specs = (
        P(("parts", "beam"), None, "head"),
        P("head"),
        P(None, ("parts", "beam"), "head"),
        P(None, ("parts", "beam"), "head"),
        P(None, ("parts", "beam"), "head"),
        P(None, ("parts", "beam"), "head"),
        P(None, "parts"),
        P("head", "beam"),
    )
    out_specs = (P(None, ("parts", "head"), "beam"), P(("parts", "beam"), None, "head"))
    return jax.shard_map(shards, mesh=mesh, in_specs=in_specs, out_specs=out_specs, check_vma=False)
```

```python
import functools

import jax
import jax.numpy as jnp
from jax import lax
from jax.experimental import pallas as pl
from jax.experimental.pallas import tpu as pltpu
from jax.sharding import PartitionSpec as P

F32, BF16 = jnp.float32, jnp.bfloat16
VMEM = pl.BlockSpec(memory_space=pltpu.VMEM)
SMEM = pl.BlockSpec(memory_space=pltpu.SMEM)
ANY = pl.BlockSpec(memory_space=pl.ANY)
STEPS, ARRAYS = 2, 4
Q, K, V, G = range(ARRAYS)
EXTRA = 16
KEPT = 8


def params(limit=48):
    return pltpu.CompilerParams(vmem_limit_bytes=limit << 20)


def cost(flops, moved):
    return pl.CostEstimate(flops=flops, bytes_accessed=moved, transcendentals=0)


def row_of(head, array, step):
    return head * ARRAYS * STEPS + array * STEPS + step


def by_partner(order, refs):
    return [ref for _, ref in sorted(zip(order, refs), key=lambda pair: pair[0])]


def pack_kernel(n, order, st_hbm, q, k, v, g, parents_hbm, *rest):
    outs, (parents, st, vectors, rows, sem, sem_small) = by_partner(order, rest[:n]), rest[n:]
    slots, dim, columns = st.shape
    heads = columns // dim // n
    me = lax.axis_index("beam")

    def lanes(head, count):
        return pl.ds(pl.multiple_of(head * dim, dim), count * dim)

    small = [pltpu.make_async_copy(ref, vectors.at[a], sem_small.at[a]) for a, ref in enumerate((q, k, v, g))]
    small.append(pltpu.make_async_copy(parents_hbm, parents, sem_small.at[ARRAYS]))
    large = {}
    for x in order:
        at = lanes((me ^ x) * heads, heads)
        large[x] = pltpu.make_async_copy(st_hbm.at[:, :, at], st.at[:, :, at], sem.at[x])
    for c in small + list(large.values()):
        c.start()
    for a in range(ARRAYS):
        small[a].wait()
        whole = vectors[a].astype(F32)
        for t in range(STEPS):
            for j in range(slots):
                rows[j, a * STEPS + t : a * STEPS + t + 1, :] = whole[t, j : j + 1]
    for x in order:
        large[x].wait()
        first = (me ^ x) * heads
        for j in range(slots):
            extra = []
            for i in range(heads):
                at = lanes(first + i, 1)
                outs[x][j, i * dim : (i + 1) * dim, :] = st[j, :, at].astype(BF16)
                extra.append(rows[j, :, at])
            outs[x][j, heads * dim :, :] = jnp.concatenate(extra, 0).astype(BF16)
    small[ARRAYS].wait()


def middle_kernel(n, order, parents, decay, *rest):
    ins, outs, (buf, vectors, kept) = by_partner(order, rest[:n]), by_partner(order, rest[n : 2 * n]), rest[2 * n :]
    slots, rows, dim = ins[0].shape
    depth = rows - EXTRA
    heads = depth // dim
    total = n * slots
    me = lax.axis_index("beam")
    for x in range(n):
        for j in range(slots):
            slot = (me ^ x) * slots + j
            buf[slot] = ins[x][j, :depth, :]
            at = pl.multiple_of(slot * EXTRA, EXTRA)
            vectors[pl.ds(at, EXTRA), :] = ins[x][j, depth:, :].astype(F32)
    for x in range(n):
        for j in range(slots):
            middle = parents[1, (me ^ x) * slots + j]
            outs[x][j * depth : (j + 1) * depth, :] = buf[parents[0, middle]]
            for i in range(heads):
                for place, array in enumerate((K, V)):
                    to = j * KEPT + i * 2 + place
                    kept[to : to + 1, :] = vectors[pl.ds(middle * EXTRA + row_of(i, array, 0), 1), :]
        outs[x][slots * depth : slots * (depth + KEPT), :] = kept[...].astype(BF16)
    line = lax.broadcasted_iota(jnp.int32, (STEPS * total, dim), 0)
    mid_line = lax.broadcasted_iota(jnp.int32, (total, total), 0)
    source = jnp.zeros((STEPS * total, dim), jnp.int32)
    chosen = jnp.zeros((total, total), jnp.int32)
    for c in range(total):
        middle = parents[1, c]
        source = jnp.where(line == c, parents[0, c], source)
        source = jnp.where(line == total + c, parents[0, middle], source)
        chosen = jnp.where(mid_line == c, middle, chosen)
    pick = (chosen == lax.broadcasted_iota(jnp.int32, (total, total), 1)).astype(BF16)
    for i in range(heads):
        d = decay[pl.ds(me * heads + i, 1), :]

        def get(array, step):
            return vectors[pl.ds(row_of(i, array, step), total, stride=EXTRA), :]

        q1, q2, k1, k2 = get(Q, 0), get(Q, 1), get(K, 0), get(K, 1)
        v1, v2 = get(V, 0), get(V, 1)
        queries = jnp.concatenate([q1, q2], 0)
        acc = jnp.zeros((STEPS * total, dim), F32)
        for slot in range(total):
            mine = jnp.where(source == slot, queries, 0.0).astype(BF16)
            acc += jnp.dot(mine, buf[slot, i * dim : (i + 1) * dim, :], preferred_element_type=F32)
        k1m = jnp.dot(pick, k1.astype(BF16), preferred_element_type=F32)
        v1m = jnp.dot(pick, v1.astype(BF16), preferred_element_type=F32)
        r1 = d * acc[:total] + jnp.sum(q1 * k1, -1, keepdims=True) * v1
        r2 = d * (d * acc[total:] + jnp.sum(q2 * k1m, -1, keepdims=True) * v1m)
        r2 = r2 + jnp.sum(q2 * k2, -1, keepdims=True) * v2
        attn = [jax.nn.sigmoid(get(G, 0)) * r1, jax.nn.sigmoid(get(G, 1)) * r2]
        attn = jnp.concatenate(attn, 0).astype(BF16)
        at = slots * (depth + KEPT) + i * STEPS * total
        for x in range(n):
            outs[x][at : at + STEPS * total, :] = attn


def project_kernel(n, order, head_count, slots, weight, *rest):
    ins, (keep, send, terms) = by_partner(order, rest[:n]), rest[n:]
    me, head = lax.axis_index("beam"), lax.axis_index("head")
    lines, dim = terms.shape[0], ins[0].shape[1]
    heads = weight.shape[0] // dim // n
    first = slots * (heads * dim + KEPT)
    acc = None
    for x in range(n):
        rows = pl.ds(pl.multiple_of((me ^ x) * heads * dim, dim), heads * dim)
        lhs = [ins[x][first + i * lines : first + (i + 1) * lines, :] for i in range(heads)]
        term = jnp.dot(jnp.concatenate(lhs, 1), weight[rows, :], preferred_element_type=F32)
        acc = term if acc is None else acc + term
    terms[...] = acc
    part = lines // STEPS // head_count
    for t in range(STEPS):
        own = pl.multiple_of(t * part * head_count + head * part, part)
        other = pl.multiple_of(t * part * head_count + (1 - head) * part, part)
        keep[t] = terms[pl.ds(own, part), :]
        send[t] = terms[pl.ds(other, part), :]


def final_kernel(n, order, decay, k, v, *rest):
    ins, (out, ks, vs) = by_partner(order, rest[:n]), rest[n:]
    slots, dim, columns = out.shape
    heads = columns // dim // n
    depth = heads * dim
    me = lax.axis_index("beam")
    ks[...] = k[1].astype(F32)
    vs[...] = v[1].astype(F32)
    line = lax.broadcasted_iota(jnp.int32, (16, dim), 0)
    for x in range(n):
        extra = ins[x][slots * depth : slots * (depth + KEPT), :].astype(F32)
        for j in range(slots):
            for i in range(heads):
                h = (me ^ x) * heads + i
                d = decay[pl.ds(h, 1), :]
                at = pl.ds(pl.multiple_of(h * dim, dim), dim)
                row = j * KEPT + i * 2
                k1, v1 = extra[row : row + 1], extra[row + 1 : row + 2]
                scaled = d * v1
                high = scaled.astype(BF16).astype(F32)
                low = scaled - high
                lhs = jnp.where(line < 2, k1, jnp.where(line == 2, ks[j : j + 1, at], 0.0))
                rhs = jnp.where(line == 0, high, jnp.where(line == 1, low, vs[j : j + 1, at]))
                outer = lax.dot_general(
                    lhs.astype(BF16), rhs.astype(BF16), (((0,), (0,)), ((), ())), preferred_element_type=F32
                )
                first = j * depth + i * dim
                out[j, :, at] = (d * d) * ins[x][first : first + dim, :].astype(F32) + outer


def fast(n, head_count, states, decay_rates, queries, key_vectors, values, gate_logits, parents, out_weight):
    slots, dim, columns = states.shape
    heads = columns // dim // n
    total, depth = n * slots, heads * dim
    order = [1, 4, 5, 6, 7, 2, 3, 0]
    decay = jnp.broadcast_to(jnp.exp(-decay_rates)[:, None], (columns // dim, dim))

    def exchange(chunks):
        return [
            lax.ppermute(chunk, "beam", [(j, j ^ x) for j in range(n)]) if x else chunk
            for x, chunk in zip(order, chunks)
        ]

    *packed, table = pl.pallas_call(
        functools.partial(pack_kernel, n, order),
        out_shape=[jax.ShapeDtypeStruct((slots, depth + EXTRA, dim), BF16)] * n
        + [jax.ShapeDtypeStruct(parents.shape, jnp.int32)],
        in_specs=[ANY] * 6,
        out_specs=[VMEM] * n + [SMEM],
        scratch_shapes=[
            pltpu.VMEM((slots, dim, columns), F32),
            pltpu.VMEM((ARRAYS, *queries.shape), BF16),
            pltpu.VMEM((slots, ARRAYS * STEPS, columns), F32),
            pltpu.SemaphoreType.DMA((n,)),
            pltpu.SemaphoreType.DMA((ARRAYS + 1,)),
        ],
    )(states, queries, key_vectors, values, gate_logits, parents)
    lines = slots * (depth + KEPT) + heads * STEPS * total
    picked = pl.pallas_call(
        functools.partial(middle_kernel, n, order),
        out_shape=[jax.ShapeDtypeStruct((lines, dim), BF16)] * n,
        in_specs=[SMEM] + [VMEM] * (n + 1),
        out_specs=[VMEM] * n,
        scratch_shapes=[
            pltpu.VMEM((total, depth, dim), BF16),
            pltpu.VMEM((total * EXTRA, dim), F32),
            pltpu.VMEM((slots * KEPT, dim), F32),
        ],
        compiler_params=params(),
    )(table, decay, *exchange(packed))
    forked = exchange(picked)
    piece = jax.ShapeDtypeStruct((STEPS, total // head_count, out_weight.shape[1]), F32)
    keep, send = pl.pallas_call(
        functools.partial(project_kernel, n, order, head_count, slots),
        out_shape=[piece, piece],
        in_specs=[VMEM] * (n + 1),
        out_specs=[VMEM] * 2,
        scratch_shapes=[pltpu.VMEM((STEPS * total, out_weight.shape[1]), F32)],
        compiler_params=params(),
    )(out_weight, *forked)
    other = lax.ppermute(send, "head", [(0, 1), (1, 0)])
    projected = (keep + other).astype(BF16)
    final = pl.pallas_call(
        functools.partial(final_kernel, n, order),
        out_shape=jax.ShapeDtypeStruct(states.shape, F32),
        in_specs=[VMEM] + [VMEM] * (n + 2),
        out_specs=VMEM,
        scratch_shapes=[pltpu.VMEM((slots, columns), F32)] * 2,
        compiler_params=params(),
        cost_estimate=cost(1 << 31, 1 << 20),
    )(decay, key_vectors, values, *forked)
    return projected, final


def fork(state, parent_list):
    row_state = lax.all_to_all(state, "beam", split_axis=1, concat_axis=0, tiled=True)
    picked = jnp.take(row_state, parent_list, axis=0)
    return lax.all_to_all(picked, "beam", split_axis=0, concat_axis=1, tiled=True)


def general(states, decay_rates, queries, key_vectors, values, gate_logits, parents, out_weight):
    slot_count, head_dim, columns = states.shape
    groups = columns // head_dim
    decay = jnp.exp(-decay_rates)
    current = states
    readouts = []
    for step in range(parents.shape[0]):
        forked = fork(current, parents[step])
        query_f = queries[step].astype(F32).reshape(slot_count, groups, head_dim)
        key_f = key_vectors[step].astype(F32).reshape(slot_count, groups, head_dim)
        value_f = values[step].astype(F32).reshape(slot_count, groups, head_dim)
        grid = forked.reshape(slot_count, head_dim, groups, head_dim)
        updated = decay[None, None, :, None] * grid + jnp.einsum("shi,shj->sihj", key_f, value_f)
        readout = jnp.einsum("shi,sihj->shj", query_f, updated, precision=lax.Precision.HIGHEST)
        current = updated.reshape(slot_count, head_dim, columns)
        readouts.append(readout.reshape(slot_count, columns))
    stacked = jnp.stack(readouts)
    attn = (jax.nn.sigmoid(gate_logits.astype(F32)) * stacked).astype(BF16)
    terms = jnp.einsum(
        "tsc,cd->tsd",
        lax.all_gather(attn, "beam", axis=1, tiled=True),
        out_weight,
        preferred_element_type=F32,
    )
    projected = lax.psum_scatter(terms, "head", scatter_dimension=1, tiled=True).astype(BF16)
    return (projected, current)


def solution(mesh):
    n, head_count = mesh.shape["beam"], mesh.shape["head"]

    def shards(*args):
        columns, dim = args[0].shape[2], args[0].shape[1]
        if n & (n - 1) == 0 and columns // dim == 2 * n and head_count == 2:
            return fast(n, head_count, *args)
        return general(*args)

    in_specs = (
        P(("parts", "beam"), None, "head"),
        P("head"),
        P(None, ("parts", "beam"), "head"),
        P(None, ("parts", "beam"), "head"),
        P(None, ("parts", "beam"), "head"),
        P(None, ("parts", "beam"), "head"),
        P(None, "parts"),
        P("head", "beam"),
    )
    out_specs = (P(None, ("parts", "head"), "beam"), P(("parts", "beam"), None, "head"))
    return jax.shard_map(shards, mesh=mesh, in_specs=in_specs, out_specs=out_specs, check_vma=False)
```

```python
import functools

import jax
import jax.numpy as jnp
from jax import lax
from jax.experimental import pallas as pl
from jax.experimental.pallas import tpu as pltpu
from jax.sharding import PartitionSpec as P

F32, BF16 = jnp.float32, jnp.bfloat16
VMEM = pl.BlockSpec(memory_space=pltpu.VMEM)
SMEM = pl.BlockSpec(memory_space=pltpu.SMEM)
ANY = pl.BlockSpec(memory_space=pl.ANY)
STEPS, ARRAYS = 2, 4
Q, K, V, G = range(ARRAYS)
EXTRA = 16
KEPT = 8


def params(limit=48):
    return pltpu.CompilerParams(vmem_limit_bytes=limit << 20)


def cost(flops, moved):
    return pl.CostEstimate(flops=flops, bytes_accessed=moved, transcendentals=0)


def row_of(head, array, step):
    return head * ARRAYS * STEPS + array * STEPS + step


def by_partner(order, refs):
    return [ref for _, ref in sorted(zip(order, refs), key=lambda pair: pair[0])]


def pack_kernel(n, order, st_hbm, q, k, v, g, *rest):
    outs, (st, vectors, rows, chunk, sem, sem_small, sem_out) = dict(zip(order, rest)), rest[-7:]
    slots, dim, columns = st.shape
    heads = columns // dim // n
    me = lax.axis_index("beam")

    def lanes(head, count):
        return pl.ds(pl.multiple_of(head * dim, dim), count * dim)

    small = [pltpu.make_async_copy(ref, vectors.at[a], sem_small.at[a]) for a, ref in enumerate((q, k, v, g))]
    large = {}
    for x in order:
        at = lanes((me ^ x) * heads, heads)
        large[x] = pltpu.make_async_copy(st_hbm.at[:, :, at], st.at[:, :, at], sem.at[x])
    for c in small + list(large.values()):
        c.start()
    for a in range(ARRAYS):
        small[a].wait()
        whole = vectors[a].astype(F32)
        for t in range(STEPS):
            for j in range(slots):
                rows[j, a * STEPS + t : a * STEPS + t + 1, :] = whole[t, j : j + 1]
    for x in order:
        large[x].wait()
        first = (me ^ x) * heads
        for j in range(slots):
            extra = []
            for i in range(heads):
                at = lanes(first + i, 1)
                chunk[x, j, i * dim : (i + 1) * dim, :] = st[j, :, at].astype(BF16)
                extra.append(rows[j, :, at])
            chunk[x, j, heads * dim :, :] = jnp.concatenate(extra, 0).astype(BF16)
        large[x] = pltpu.make_async_copy(chunk.at[x], outs[x], sem_out.at[x])
        large[x].start()
    for x in order:
        large[x].wait()


def hold_kernel(chunk, out):
    out[...] = chunk[...]


def middle_kernel(n, first, second, parents_hbm, decay, *rest):
    ins, outs = by_partner(first, rest[:n]), by_partner(second, rest[n : 2 * n])
    buf, vectors, kept, parents, own, sem = rest[2 * n :]
    copies = [pltpu.make_async_copy(parents_hbm, parents, sem.at[0]), pltpu.make_async_copy(ins[0], own, sem.at[1])]
    for c in copies:
        c.start()
    ins[0] = own
    slots, rows, dim = own.shape
    depth = rows - EXTRA
    heads = depth // dim
    total = n * slots
    me = lax.axis_index("beam")
    for x in [*range(1, n), 0]:
        if x == 0:
            for c in copies:
                c.wait()
        for j in range(slots):
            slot = (me ^ x) * slots + j
            buf[slot] = ins[x][j, :depth, :]
            at = pl.multiple_of(slot * EXTRA, EXTRA)
            vectors[pl.ds(at, EXTRA), :] = ins[x][j, depth:, :].astype(F32)
    for x in range(n):
        for j in range(slots):
            middle = parents[1, (me ^ x) * slots + j]
            outs[x][j * depth : (j + 1) * depth, :] = buf[parents[0, middle]]
            for i in range(heads):
                for place, array in enumerate((K, V)):
                    to = j * KEPT + i * 2 + place
                    kept[to : to + 1, :] = vectors[pl.ds(parents[STEPS + 1, (me ^ x) * slots + j] + row_of(i, array, 0), 1), :]
        outs[x][slots * depth : slots * (depth + KEPT), :] = kept[...].astype(BF16)
    line = lax.broadcasted_iota(jnp.int32, (STEPS * total, dim), 0)
    mid_line = lax.broadcasted_iota(jnp.int32, (total, total), 0)
    source = jnp.zeros((STEPS * total, dim), jnp.int32)
    chosen = jnp.zeros((total, total), jnp.int32)
    for c in range(total):
        middle = parents[1, c]
        source = jnp.where(line == c, parents[0, c], source)
        source = jnp.where(line == total + c, parents[0, middle], source)
        chosen = jnp.where(mid_line == c, middle, chosen)
    pick = (chosen == lax.broadcasted_iota(jnp.int32, (total, total), 1)).astype(BF16)
    for i in range(heads):
        d = decay[pl.ds(me * heads + i, 1), :]

        def get(array, step):
            return vectors[pl.ds(row_of(i, array, step), total, stride=EXTRA), :]

        q1, q2, k1, k2 = get(Q, 0), get(Q, 1), get(K, 0), get(K, 1)
        v1, v2 = get(V, 0), get(V, 1)
        queries = jnp.concatenate([q1, q2], 0)
        acc = jnp.zeros((STEPS * total, dim), F32)
        for slot in range(total):
            mine = jnp.where(source == slot, queries, 0.0).astype(BF16)
            acc += jnp.dot(mine, buf[slot, i * dim : (i + 1) * dim, :], preferred_element_type=F32)
        k1m = jnp.dot(pick, k1.astype(BF16), preferred_element_type=F32)
        v1m = jnp.dot(pick, v1.astype(BF16), preferred_element_type=F32)
        r1 = d * acc[:total] + jnp.sum(q1 * k1, -1, keepdims=True) * v1
        r2 = d * (d * acc[total:] + jnp.sum(q2 * k1m, -1, keepdims=True) * v1m)
        r2 = r2 + jnp.sum(q2 * k2, -1, keepdims=True) * v2
        attn = [jax.nn.sigmoid(get(G, 0)) * r1, jax.nn.sigmoid(get(G, 1)) * r2]
        attn = jnp.concatenate(attn, 0).astype(BF16)
        at = slots * (depth + KEPT) + i * STEPS * total
        for x in range(n):
            outs[x][at : at + STEPS * total, :] = attn


def project_kernel(n, order, head_count, slots, weight, *rest):
    ins, (keep, send, terms) = by_partner(order, rest[:n]), rest[n + 1 :]
    me, head = lax.axis_index("beam"), lax.axis_index("head")
    lines, dim = terms.shape[0], ins[0].shape[1]
    heads = weight.shape[0] // dim // n
    first = slots * (heads * dim + KEPT)
    acc = None
    for x in range(n):
        rows = pl.ds(pl.multiple_of((me ^ x) * heads * dim, dim), heads * dim)
        lhs = [ins[x][first + i * lines : first + (i + 1) * lines, :] for i in range(heads)]
        term = jnp.dot(jnp.concatenate(lhs, 1), weight[rows, :], preferred_element_type=F32)
        acc = term if acc is None else acc + term
    terms[...] = acc
    part = lines // STEPS // head_count
    for t in range(STEPS):
        own = pl.multiple_of(t * part * head_count + head * part, part)
        other = pl.multiple_of(t * part * head_count + (1 - head) * part, part)
        keep[t] = terms[pl.ds(own, part), :]
        send[t] = terms[pl.ds(other, part), :]


def final_kernel(n, order, first, decay, k, v, *rest):
    ins, (result, *token, out, ks, vs, sem) = dict(zip(order, rest)), rest[-5 - first :]
    if first:
        token[0][...] = jnp.zeros_like(token[0])
    slots, dim, columns = result.shape
    heads = columns // dim // n
    depth = heads * dim
    me = lax.axis_index("beam")
    ks[...] = k[1].astype(F32)
    vs[...] = v[1].astype(F32)
    line = lax.broadcasted_iota(jnp.int32, (16, dim), 0)
    copies = []
    for x in order:
        extra = ins[x][slots * depth : slots * (depth + KEPT), :].astype(F32)
        for j in range(slots):
            for i in range(heads):
                h = (me ^ x) * heads + i
                d = decay[pl.ds(h, 1), :]
                at = pl.ds(pl.multiple_of(h * dim, dim), dim)
                row = j * KEPT + i * 2
                k1, v1 = extra[row : row + 1], extra[row + 1 : row + 2]
                scaled = d * v1
                high = scaled.astype(BF16).astype(F32)
                low = scaled - high
                lhs = jnp.where(line < 2, k1, jnp.where(line == 2, ks[j : j + 1, at], 0.0))
                rhs = jnp.where(line == 0, high, jnp.where(line == 1, low, vs[j : j + 1, at]))
                outer = lax.dot_general(
                    lhs.astype(BF16), rhs.astype(BF16), (((0,), (0,)), ((), ())), preferred_element_type=F32
                )
                first = j * depth + i * dim
                out[j, :, at] = (d * d) * ins[x][first : first + dim, :].astype(F32) + outer
        at = pl.ds(pl.multiple_of((me ^ x) * depth, depth), depth)
        copies.append(pltpu.make_async_copy(out.at[:, :, at], result.at[:, :, at], sem.at[x]))
        copies[-1].start()
    for c in copies:
        c.wait()


def fast(n, head_count, states, decay_rates, queries, key_vectors, values, gate_logits, parents, out_weight):
    slots, dim, columns = states.shape
    heads = columns // dim // n
    total, depth = n * slots, heads * dim
    first, second = [4, 1, 2, 5, 3, 6, 7, 0], [4, 1, 2, 5, 3, 6, 7, 0]
    decay = jnp.broadcast_to(jnp.exp(-decay_rates)[:, None], (columns // dim, dim))

    def exchange(order, chunks):
        return [
            lax.ppermute(chunk, "beam", [(j, j ^ x) for j in range(n)]) if x else chunk
            for x, chunk in zip(order, chunks)
        ]

    table = jnp.concatenate([parents, parents * EXTRA], 0)
    packed = []
    for part in (first[:1], first[1:]):
        packed += pl.pallas_call(
            functools.partial(pack_kernel, n, part),
            out_shape=[jax.ShapeDtypeStruct((slots, depth + EXTRA, dim), BF16)] * len(part),
            in_specs=[ANY] * 5,
            out_specs=[ANY] * len(part),
            scratch_shapes=[
                pltpu.VMEM((slots, dim, columns), F32),
                pltpu.VMEM((ARRAYS, *queries.shape), BF16),
                pltpu.VMEM((slots, ARRAYS * STEPS, columns), F32),
                pltpu.VMEM((n, slots, depth + EXTRA, dim), BF16),
                pltpu.SemaphoreType.DMA((n,)),
                pltpu.SemaphoreType.DMA((ARRAYS,)),
                pltpu.SemaphoreType.DMA((n,)),
            ],
        )(states, queries, key_vectors, values, gate_logits)
    packed[-1] = pl.pallas_call(
        hold_kernel,
        out_shape=jax.ShapeDtypeStruct(packed[-1].shape, BF16),
        in_specs=[VMEM],
        out_specs=VMEM,
        compiler_params=params(),
    )(packed[-1])
    lines = slots * (depth + KEPT) + heads * STEPS * total
    picked = pl.pallas_call(
        functools.partial(middle_kernel, n, first, second),
        out_shape=[jax.ShapeDtypeStruct((lines, dim), BF16)] * n,
        in_specs=[ANY] + [VMEM] * n + [ANY],
        out_specs=[VMEM] * n,
        scratch_shapes=[
            pltpu.VMEM((total, depth, dim), BF16),
            pltpu.VMEM((total * EXTRA, dim), F32),
            pltpu.VMEM((slots * KEPT, dim), F32),
            pltpu.SMEM(table.shape, jnp.int32),
            pltpu.VMEM((slots, depth + EXTRA, dim), BF16),
            pltpu.SemaphoreType.DMA((2,)),
        ],
        compiler_params=params(),
    )(table, decay, *exchange(first, packed))
    forked = exchange(second, picked)
    held = dict(zip(second, forked))

    whole = jax.ShapeDtypeStruct(states.shape, F32)

    def finish(part, *before):
        return pl.pallas_call(
            functools.partial(final_kernel, n, part, not before),
            out_shape=[whole] if before else [whole, jax.ShapeDtypeStruct((8, dim), F32)],
            in_specs=[VMEM] * (len(part) + 3) + [ANY] * len(before),
            out_specs=[ANY] if before else [ANY, VMEM],
            input_output_aliases={len(part) + 3: 0} if before else {},
            scratch_shapes=[
                pltpu.VMEM(states.shape, F32),
                pltpu.VMEM((slots, columns), F32),
                pltpu.VMEM((slots, columns), F32),
                pltpu.SemaphoreType.DMA((n,)),
            ],
            compiler_params=params(),
        )(decay, key_vectors, values, *[held[x] for x in part], *before)

    begun, token = finish(second[:6] + second[-1:])
    piece = jax.ShapeDtypeStruct((STEPS, total // head_count, out_weight.shape[1]), F32)
    keep, send = pl.pallas_call(
        functools.partial(project_kernel, n, second, head_count, slots),
        out_shape=[piece, piece],
        in_specs=[VMEM] * (n + 1) + [VMEM],
        out_specs=[VMEM] * 2,
        scratch_shapes=[pltpu.VMEM((STEPS * total, out_weight.shape[1]), F32)],
        compiler_params=params(),
    )(out_weight, *forked, token)
    other = lax.ppermute(send, "head", [(0, 1), (1, 0)])
    projected = (keep + other).astype(BF16)
    (final,) = finish(second[6:-1], begun)
    return projected, final


def fork(state, parent_list):
    row_state = lax.all_to_all(state, "beam", split_axis=1, concat_axis=0, tiled=True)
    picked = jnp.take(row_state, parent_list, axis=0)
    return lax.all_to_all(picked, "beam", split_axis=0, concat_axis=1, tiled=True)


def general(states, decay_rates, queries, key_vectors, values, gate_logits, parents, out_weight):
    slot_count, head_dim, columns = states.shape
    groups = columns // head_dim
    decay = jnp.exp(-decay_rates)
    current = states
    readouts = []
    for step in range(parents.shape[0]):
        forked = fork(current, parents[step])
        query_f = queries[step].astype(F32).reshape(slot_count, groups, head_dim)
        key_f = key_vectors[step].astype(F32).reshape(slot_count, groups, head_dim)
        value_f = values[step].astype(F32).reshape(slot_count, groups, head_dim)
        grid = forked.reshape(slot_count, head_dim, groups, head_dim)
        updated = decay[None, None, :, None] * grid + jnp.einsum("shi,shj->sihj", key_f, value_f)
        readout = jnp.einsum("shi,sihj->shj", query_f, updated, precision=lax.Precision.HIGHEST)
        current = updated.reshape(slot_count, head_dim, columns)
        readouts.append(readout.reshape(slot_count, columns))
    stacked = jnp.stack(readouts)
    attn = (jax.nn.sigmoid(gate_logits.astype(F32)) * stacked).astype(BF16)
    terms = jnp.einsum(
        "tsc,cd->tsd",
        lax.all_gather(attn, "beam", axis=1, tiled=True),
        out_weight,
        preferred_element_type=F32,
    )
    projected = lax.psum_scatter(terms, "head", scatter_dimension=1, tiled=True).astype(BF16)
    return (projected, current)


def solution(mesh):
    n, head_count = mesh.shape["beam"], mesh.shape["head"]

    def shards(*args):
        columns, dim = args[0].shape[2], args[0].shape[1]
        if n & (n - 1) == 0 and columns // dim == 2 * n and head_count == 2:
            return fast(n, head_count, *args)
        return general(*args)

    in_specs = (
        P(("parts", "beam"), None, "head"),
        P("head"),
        P(None, ("parts", "beam"), "head"),
        P(None, ("parts", "beam"), "head"),
        P(None, ("parts", "beam"), "head"),
        P(None, ("parts", "beam"), "head"),
        P(None, "parts"),
        P("head", "beam"),
    )
    out_specs = (P(None, ("parts", "head"), "beam"), P(("parts", "beam"), None, "head"))
    return jax.shard_map(shards, mesh=mesh, in_specs=in_specs, out_specs=out_specs, check_vma=False)
```

```python
import functools

import jax
import jax.numpy as jnp
from jax import lax
from jax.experimental import pallas as pl
from jax.experimental.pallas import tpu as pltpu
from jax.sharding import PartitionSpec as P

F32, BF16 = jnp.float32, jnp.bfloat16
VMEM = pl.BlockSpec(memory_space=pltpu.VMEM)
SMEM = pl.BlockSpec(memory_space=pltpu.SMEM)
ANY = pl.BlockSpec(memory_space=pl.ANY)
STEPS, ARRAYS = 2, 4
Q, K, V, G = range(ARRAYS)
EXTRA = 16
KEPT = 8


def params(limit=48):
    return pltpu.CompilerParams(vmem_limit_bytes=limit << 20)


def cost(flops, moved):
    return pl.CostEstimate(flops=flops, bytes_accessed=moved, transcendentals=0)


def row_of(head, array, step):
    return head * ARRAYS * STEPS + array * STEPS + step


def by_partner(order, refs):
    return [ref for _, ref in sorted(zip(order, refs), key=lambda pair: pair[0])]


def pack_kernel(n, order, st_hbm, q, k, v, g, *rest):
    outs, (st, vectors, rows, chunk, sem, sem_small, sem_out) = dict(zip(order, rest)), rest[-7:]
    slots, dim, columns = st.shape
    heads = columns // dim // n
    me = lax.axis_index("beam")

    def lanes(head, count):
        return pl.ds(pl.multiple_of(head * dim, dim), count * dim)

    at = lanes((me ^ order[0]) * heads, heads) if len(order) == 1 else slice(None)
    small = [
        pltpu.make_async_copy(ref.at[:, :, at], vectors.at[a, :, :, at], sem_small.at[a])
        for a, ref in enumerate((q, k, v, g))
    ]
    large = {}
    for x in order:
        here = lanes((me ^ x) * heads, heads)
        large[x] = pltpu.make_async_copy(st_hbm.at[:, :, here], st.at[:, :, here], sem.at[x])
    for c in [large[order[0]], *small, *list(large.values())[1:]]:
        c.start()
    for a in range(ARRAYS):
        small[a].wait()
        whole = vectors[a, :, :, at].astype(F32)
        for t in range(STEPS):
            for j in range(slots):
                rows[j, a * STEPS + t : a * STEPS + t + 1, at] = whole[t, j : j + 1]
    for x in order:
        large[x].wait()
        first = (me ^ x) * heads
        for j in range(slots):
            extra = []
            for i in range(heads):
                at = lanes(first + i, 1)
                chunk[x, j, i * dim : (i + 1) * dim, :] = st[j, :, at].astype(BF16)
                extra.append(rows[j, :, at])
            chunk[x, j, heads * dim :, :] = jnp.concatenate(extra, 0).astype(BF16)
        large[x] = pltpu.make_async_copy(chunk.at[x], outs[x], sem_out.at[x])
        large[x].start()
    for x in order:
        large[x].wait()


def hold_kernel(chunk, out):
    out[...] = chunk[...]


def middle_kernel(n, first, second, parents_hbm, decay, *rest):
    ins, outs = by_partner(first, rest[:n]), by_partner(second, rest[n : 2 * n])
    buf, vectors, kept, parents, own, sem = rest[2 * n :]
    copies = [pltpu.make_async_copy(parents_hbm, parents, sem.at[0]), pltpu.make_async_copy(ins[0], own, sem.at[1])]
    for c in copies:
        c.start()
    ins[0] = own
    slots, rows, dim = own.shape
    depth = rows - EXTRA
    heads = depth // dim
    total = n * slots
    me = lax.axis_index("beam")
    for x in [*range(1, n), 0]:
        if x == 0:
            for c in copies:
                c.wait()
        for j in range(slots):
            slot = (me ^ x) * slots + j
            for i in range(heads):
                to = pl.ds(pl.multiple_of(slot * dim, dim), dim)
                buf[i, to, :] = ins[x][j, i * dim : (i + 1) * dim, :]
            at = pl.multiple_of(slot * EXTRA, EXTRA)
            vectors[pl.ds(at, EXTRA), :] = ins[x][j, depth:, :].astype(F32)
    for x in range(n):
        for j in range(slots):
            middle = parents[1, (me ^ x) * slots + j]
            root = pl.ds(pl.multiple_of(parents[0, middle] * dim, dim), dim)
            for i in range(heads):
                outs[x][j * depth + i * dim : j * depth + (i + 1) * dim, :] = buf[i, root, :]
            for i in range(heads):
                for place, array in enumerate((K, V)):
                    to = j * KEPT + i * 2 + place
                    kept[to : to + 1, :] = vectors[pl.ds(parents[STEPS + 1, (me ^ x) * slots + j] + row_of(i, array, 0), 1), :]
        outs[x][slots * depth : slots * (depth + KEPT), :] = kept[...].astype(BF16)
    line = lax.broadcasted_iota(jnp.int32, (STEPS * total, dim), 0)
    mid_line = lax.broadcasted_iota(jnp.int32, (total, total), 0)
    source = jnp.zeros((STEPS * total, dim), jnp.int32)
    chosen = jnp.zeros((total, total), jnp.int32)
    for c in range(total):
        middle = parents[1, c]
        source = jnp.where(line == c, parents[0, c], source)
        source = jnp.where(line == total + c, parents[0, middle], source)
        chosen = jnp.where(mid_line == c, middle, chosen)
    pick = (chosen == lax.broadcasted_iota(jnp.int32, (total, total), 1)).astype(BF16)
    for i in range(heads):
        d = decay[pl.ds(me * heads + i, 1), :]

        def get(array, step):
            return vectors[pl.ds(row_of(i, array, step), total, stride=EXTRA), :]

        q1, q2, k1, k2 = get(Q, 0), get(Q, 1), get(K, 0), get(K, 1)
        v1, v2 = get(V, 0), get(V, 1)
        queries = jnp.concatenate([q1, q2], 0)
        mine = [jnp.where(source == slot, queries, 0.0).astype(BF16) for slot in range(total)]
        acc = jnp.dot(jnp.concatenate(mine, 1), buf[i], preferred_element_type=F32)
        k1m = jnp.dot(pick, k1.astype(BF16), preferred_element_type=F32)
        v1m = jnp.dot(pick, v1.astype(BF16), preferred_element_type=F32)
        r1 = d * acc[:total] + jnp.sum(q1 * k1, -1, keepdims=True) * v1
        r2 = d * (d * acc[total:] + jnp.sum(q2 * k1m, -1, keepdims=True) * v1m)
        r2 = r2 + jnp.sum(q2 * k2, -1, keepdims=True) * v2
        attn = [jax.nn.sigmoid(get(G, 0)) * r1, jax.nn.sigmoid(get(G, 1)) * r2]
        attn = jnp.concatenate(attn, 0).astype(BF16)
        at = slots * (depth + KEPT) + i * STEPS * total
        for x in range(n):
            outs[x][at : at + STEPS * total, :] = attn


def project(n, slots, lines, weight, ins):
    me = lax.axis_index("beam")
    dim = next(iter(ins.values())).shape[1]
    heads = weight.shape[0] // dim // n
    first = slots * (heads * dim + KEPT)
    acc = None
    for x, ref in ins.items():
        rows = pl.ds(pl.multiple_of((me ^ x) * heads * dim, dim), heads * dim)
        lhs = [ref[first + i * lines : first + (i + 1) * lines, :] for i in range(heads)]
        term = jnp.dot(jnp.concatenate(lhs, 1), weight[rows, :], preferred_element_type=F32)
        acc = term if acc is None else acc + term
    return acc


def project_kernel(n, order, head_count, slots, weight, begun, *rest):
    ins, (keep, send, terms) = dict(zip(order, rest)), rest[len(order) :]
    head, lines = lax.axis_index("head"), terms.shape[0]
    terms[...] = begun[...] + project(n, slots, lines, weight, ins)
    part = lines // STEPS // head_count
    for t in range(STEPS):
        own = pl.multiple_of(t * part * head_count + head * part, part)
        other = pl.multiple_of(t * part * head_count + (1 - head) * part, part)
        keep[t] = terms[pl.ds(own, part), :]
        send[t] = terms[pl.ds(other, part), :]


def final_kernel(n, order, first, decay, k, v, *rest):
    if first:
        weight, *rest = rest
    ins, (result, *terms, out, ks, vs, sem) = dict(zip(order, rest)), rest[-5 - first :]
    slots, dim, columns = result.shape
    if first:
        terms[0][...] = project(n, slots, terms[0].shape[0], weight, ins)
    heads = columns // dim // n
    depth = heads * dim
    me = lax.axis_index("beam")
    ks[...] = k[1].astype(F32)
    vs[...] = v[1].astype(F32)
    line = lax.broadcasted_iota(jnp.int32, (16, dim), 0)
    copies = []
    for x in order:
        extra = ins[x][slots * depth : slots * (depth + KEPT), :].astype(F32)
        for j in range(slots):
            for i in range(heads):
                h = (me ^ x) * heads + i
                d = decay[pl.ds(h, 1), :]
                at = pl.ds(pl.multiple_of(h * dim, dim), dim)
                row = j * KEPT + i * 2
                k1, v1 = extra[row : row + 1], extra[row + 1 : row + 2]
                scaled = d * v1
                high = scaled.astype(BF16).astype(F32)
                low = scaled - high
                lhs = jnp.where(line < 2, k1, jnp.where(line == 2, ks[j : j + 1, at], 0.0))
                rhs = jnp.where(line == 0, high, jnp.where(line == 1, low, vs[j : j + 1, at]))
                outer = lax.dot_general(
                    lhs.astype(BF16), rhs.astype(BF16), (((0,), (0,)), ((), ())), preferred_element_type=F32
                )
                first = j * depth + i * dim
                out[j, :, at] = (d * d) * ins[x][first : first + dim, :].astype(F32) + outer
        at = pl.ds(pl.multiple_of((me ^ x) * depth, depth), depth)
        copies.append(pltpu.make_async_copy(out.at[:, :, at], result.at[:, :, at], sem.at[x]))
        copies[-1].start()
    for c in copies:
        c.wait()


def fast(n, head_count, states, decay_rates, queries, key_vectors, values, gate_logits, parents, out_weight):
    slots, dim, columns = states.shape
    heads = columns // dim // n
    total, depth = n * slots, heads * dim
    first, second = [4, 1, 2, 5, 3, 6, 7, 0], [4, 1, 2, 5, 3, 6, 7, 0]
    decay = jnp.broadcast_to(jnp.exp(-decay_rates)[:, None], (columns // dim, dim))

    def exchange(order, chunks):
        return [
            lax.ppermute(chunk, "beam", [(j, j ^ x) for j in range(n)]) if x else chunk
            for x, chunk in zip(order, chunks)
        ]

    table = jnp.concatenate([parents, parents * EXTRA], 0)
    packed = []
    for part in (first[:1], first[1:]):
        packed += pl.pallas_call(
            functools.partial(pack_kernel, n, part),
            out_shape=[jax.ShapeDtypeStruct((slots, depth + EXTRA, dim), BF16)] * len(part),
            in_specs=[ANY] * 5,
            out_specs=[ANY] * len(part),
            scratch_shapes=[
                pltpu.VMEM((slots, dim, columns), F32),
                pltpu.VMEM((ARRAYS, *queries.shape), BF16),
                pltpu.VMEM((slots, ARRAYS * STEPS, columns), F32),
                pltpu.VMEM((n, slots, depth + EXTRA, dim), BF16),
                pltpu.SemaphoreType.DMA((n,)),
                pltpu.SemaphoreType.DMA((ARRAYS,)),
                pltpu.SemaphoreType.DMA((n,)),
            ],
        )(states, queries, key_vectors, values, gate_logits)
    packed[-1] = pl.pallas_call(
        hold_kernel,
        out_shape=jax.ShapeDtypeStruct(packed[-1].shape, BF16),
        in_specs=[VMEM],
        out_specs=VMEM,
        compiler_params=params(),
    )(packed[-1])
    lines = slots * (depth + KEPT) + heads * STEPS * total
    picked = pl.pallas_call(
        functools.partial(middle_kernel, n, first, second),
        out_shape=[jax.ShapeDtypeStruct((lines, dim), BF16)] * n,
        in_specs=[ANY] + [VMEM] * n + [ANY],
        out_specs=[VMEM] * n,
        scratch_shapes=[
            pltpu.VMEM((heads, total * dim, dim), BF16),
            pltpu.VMEM((total * EXTRA, dim), F32),
            pltpu.VMEM((slots * KEPT, dim), F32),
            pltpu.SMEM(table.shape, jnp.int32),
            pltpu.VMEM((slots, depth + EXTRA, dim), BF16),
            pltpu.SemaphoreType.DMA((2,)),
        ],
        compiler_params=params(),
    )(table, decay, *exchange(first, packed))
    forked = exchange(second, picked)
    held = dict(zip(second, forked))

    whole = jax.ShapeDtypeStruct(states.shape, F32)

    def finish(part, *before):
        more = [] if before else [out_weight]
        return pl.pallas_call(
            functools.partial(final_kernel, n, part, not before),
            out_shape=[whole] if before else [whole, jax.ShapeDtypeStruct((STEPS * total, out_weight.shape[1]), F32)],
            in_specs=[VMEM] * (len(more) + len(part) + 3) + [ANY] * len(before),
            out_specs=[ANY] if before else [ANY, VMEM],
            input_output_aliases={len(part) + 3: 0} if before else {},
            scratch_shapes=[
                pltpu.VMEM(states.shape, F32),
                pltpu.VMEM((slots, columns), F32),
                pltpu.VMEM((slots, columns), F32),
                pltpu.SemaphoreType.DMA((n,)),
            ],
            compiler_params=params(),
        )(decay, key_vectors, values, *more, *[held[x] for x in part], *before)

    begun, partial = finish(second[:6] + second[-1:])
    piece = jax.ShapeDtypeStruct((STEPS, total // head_count, out_weight.shape[1]), F32)
    keep, send = pl.pallas_call(
        functools.partial(project_kernel, n, second[6:-1], head_count, slots),
        out_shape=[piece, piece],
        in_specs=[VMEM] * (n + 1 - 6),
        out_specs=[VMEM] * 2,
        scratch_shapes=[pltpu.VMEM((STEPS * total, out_weight.shape[1]), F32)],
        compiler_params=params(),
    )(out_weight, partial, *forked[6:-1])
    other = lax.ppermute(send, "head", [(0, 1), (1, 0)])
    projected = (keep + other).astype(BF16)
    (final,) = finish(second[6:-1], begun)
    return projected, final


def fork(state, parent_list):
    row_state = lax.all_to_all(state, "beam", split_axis=1, concat_axis=0, tiled=True)
    picked = jnp.take(row_state, parent_list, axis=0)
    return lax.all_to_all(picked, "beam", split_axis=0, concat_axis=1, tiled=True)


def general(states, decay_rates, queries, key_vectors, values, gate_logits, parents, out_weight):
    slot_count, head_dim, columns = states.shape
    groups = columns // head_dim
    decay = jnp.exp(-decay_rates)
    current = states
    readouts = []
    for step in range(parents.shape[0]):
        forked = fork(current, parents[step])
        query_f = queries[step].astype(F32).reshape(slot_count, groups, head_dim)
        key_f = key_vectors[step].astype(F32).reshape(slot_count, groups, head_dim)
        value_f = values[step].astype(F32).reshape(slot_count, groups, head_dim)
        grid = forked.reshape(slot_count, head_dim, groups, head_dim)
        updated = decay[None, None, :, None] * grid + jnp.einsum("shi,shj->sihj", key_f, value_f)
        readout = jnp.einsum("shi,sihj->shj", query_f, updated, precision=lax.Precision.HIGHEST)
        current = updated.reshape(slot_count, head_dim, columns)
        readouts.append(readout.reshape(slot_count, columns))
    stacked = jnp.stack(readouts)
    attn = (jax.nn.sigmoid(gate_logits.astype(F32)) * stacked).astype(BF16)
    terms = jnp.einsum(
        "tsc,cd->tsd",
        lax.all_gather(attn, "beam", axis=1, tiled=True),
        out_weight,
        preferred_element_type=F32,
    )
    projected = lax.psum_scatter(terms, "head", scatter_dimension=1, tiled=True).astype(BF16)
    return (projected, current)


def solution(mesh):
    n, head_count = mesh.shape["beam"], mesh.shape["head"]

    def shards(*args):
        columns, dim = args[0].shape[2], args[0].shape[1]
        if n & (n - 1) == 0 and columns // dim == 2 * n and head_count == 2:
            return fast(n, head_count, *args)
        return general(*args)

    in_specs = (
        P(("parts", "beam"), None, "head"),
        P("head"),
        P(None, ("parts", "beam"), "head"),
        P(None, ("parts", "beam"), "head"),
        P(None, ("parts", "beam"), "head"),
        P(None, ("parts", "beam"), "head"),
        P(None, "parts"),
        P("head", "beam"),
    )
    out_specs = (P(None, ("parts", "head"), "beam"), P(("parts", "beam"), None, "head"))
    return jax.shard_map(shards, mesh=mesh, in_specs=in_specs, out_specs=out_specs, check_vma=False)
```

```python
import functools

import jax
import jax.numpy as jnp
from jax import lax
from jax.experimental import pallas as pl
from jax.experimental.pallas import tpu as pltpu
from jax.sharding import PartitionSpec as P

F32, BF16 = jnp.float32, jnp.bfloat16
VMEM = pl.BlockSpec(memory_space=pltpu.VMEM)
SMEM = pl.BlockSpec(memory_space=pltpu.SMEM)
ANY = pl.BlockSpec(memory_space=pl.ANY)
STEPS, ARRAYS = 2, 4
Q, K, V, G = range(ARRAYS)
EXTRA = 16
KEPT = 8


def params(limit=48):
    return pltpu.CompilerParams(vmem_limit_bytes=limit << 20)


def cost(flops, moved):
    return pl.CostEstimate(flops=flops, bytes_accessed=moved, transcendentals=0)


def row_of(head, array, step):
    return head * ARRAYS * STEPS + array * STEPS + step


def by_partner(order, refs):
    return [ref for _, ref in sorted(zip(order, refs), key=lambda pair: pair[0])]


def pack_kernel(n, order, st_hbm, q, k, v, g, *rest):
    outs, (st, vectors, rows, chunk, sem, sem_small, sem_out) = dict(zip(order, rest)), rest[-7:]
    slots, dim, columns = st.shape
    heads = columns // dim // n
    me = lax.axis_index("beam")

    def lanes(head, count):
        return pl.ds(pl.multiple_of(head * dim, dim), count * dim)

    at = lanes((me ^ order[0]) * heads, heads) if len(order) == 1 else slice(None)
    small = [
        pltpu.make_async_copy(ref.at[:, :, at], vectors.at[a, :, :, at], sem_small.at[a])
        for a, ref in enumerate((q, k, v, g))
    ]
    large = {}
    for x in order:
        here = lanes((me ^ x) * heads, heads)
        large[x] = pltpu.make_async_copy(st_hbm.at[:, :, here], st.at[:, :, here], sem.at[x])
    for c in [large[order[0]], *small, *list(large.values())[1:]]:
        c.start()
    for a in range(ARRAYS):
        small[a].wait()
        whole = vectors[a, :, :, at].astype(F32)
        for t in range(STEPS):
            for j in range(slots):
                rows[j, a * STEPS + t : a * STEPS + t + 1, at] = whole[t, j : j + 1]
    for x in order:
        large[x].wait()
        first = (me ^ x) * heads
        for j in range(slots):
            extra = []
            for i in range(heads):
                at = lanes(first + i, 1)
                chunk[x, j, i * dim : (i + 1) * dim, :] = st[j, :, at].astype(BF16)
                extra.append(rows[j, :, at])
            chunk[x, j, heads * dim :, :] = jnp.concatenate(extra, 0).astype(BF16)
        large[x] = pltpu.make_async_copy(chunk.at[x], outs[x], sem_out.at[x])
        large[x].start()
    for x in order:
        large[x].wait()


def hold_kernel(chunk, out):
    out[...] = chunk[...]


def middle_kernel(n, first, second, parents_hbm, decay, *rest):
    ins, outs = by_partner(first, rest[:n]), by_partner(second, rest[n : 2 * n])
    attn_out, buf, vectors, kept, parents, own, sem = rest[2 * n :]
    copies = [pltpu.make_async_copy(parents_hbm, parents, sem.at[0]), pltpu.make_async_copy(ins[0], own, sem.at[1])]
    for c in copies:
        c.start()
    ins[0] = own
    slots, rows, dim = own.shape
    depth = rows - EXTRA
    heads = depth // dim
    total = n * slots
    me = lax.axis_index("beam")
    for x in [*range(1, n), 0]:
        if x == 0:
            for c in copies:
                c.wait()
        for j in range(slots):
            slot = (me ^ x) * slots + j
            for i in range(heads):
                to = pl.ds(pl.multiple_of(slot * dim, dim), dim)
                buf[i, to, :] = ins[x][j, i * dim : (i + 1) * dim, :]
            at = pl.multiple_of(slot * EXTRA, EXTRA)
            vectors[pl.ds(at, EXTRA), :] = ins[x][j, depth:, :].astype(F32)
    for x in range(n):
        for j in range(slots):
            middle = parents[1, (me ^ x) * slots + j]
            root = pl.ds(pl.multiple_of(parents[0, middle] * dim, dim), dim)
            for i in range(heads):
                outs[x][j * depth + i * dim : j * depth + (i + 1) * dim, :] = buf[i, root, :]
            for i in range(heads):
                for place, array in enumerate((K, V)):
                    to = j * KEPT + i * 2 + place
                    kept[to : to + 1, :] = vectors[pl.ds(parents[STEPS + 1, (me ^ x) * slots + j] + row_of(i, array, 0), 1), :]
        outs[x][slots * depth : slots * (depth + KEPT), :] = kept[...].astype(BF16)
    line = lax.broadcasted_iota(jnp.int32, (STEPS * total, dim), 0)
    mid_line = lax.broadcasted_iota(jnp.int32, (total, total), 0)
    source = jnp.zeros((STEPS * total, dim), jnp.int32)
    chosen = jnp.zeros((total, total), jnp.int32)
    for c in range(total):
        middle = parents[1, c]
        source = jnp.where(line == c, parents[0, c], source)
        source = jnp.where(line == total + c, parents[0, middle], source)
        chosen = jnp.where(mid_line == c, middle, chosen)
    pick = (chosen == lax.broadcasted_iota(jnp.int32, (total, total), 1)).astype(BF16)
    for i in range(heads):
        d = decay[pl.ds(me * heads + i, 1), :]

        def get(array, step):
            return vectors[pl.ds(row_of(i, array, step), total, stride=EXTRA), :]

        q1, q2, k1, k2 = get(Q, 0), get(Q, 1), get(K, 0), get(K, 1)
        v1, v2 = get(V, 0), get(V, 1)
        queries = jnp.concatenate([q1, q2], 0)
        mine = [jnp.where(source == slot, queries, 0.0).astype(BF16) for slot in range(total)]
        acc = jnp.dot(jnp.concatenate(mine, 1), buf[i], preferred_element_type=F32)
        k1m = jnp.dot(pick, k1.astype(BF16), preferred_element_type=F32)
        v1m = jnp.dot(pick, v1.astype(BF16), preferred_element_type=F32)
        r1 = d * acc[:total] + jnp.sum(q1 * k1, -1, keepdims=True) * v1
        r2 = d * (d * acc[total:] + jnp.sum(q2 * k1m, -1, keepdims=True) * v1m)
        r2 = r2 + jnp.sum(q2 * k2, -1, keepdims=True) * v2
        attn = [jax.nn.sigmoid(get(G, 0)) * r1, jax.nn.sigmoid(get(G, 1)) * r2]
        attn = jnp.concatenate(attn, 0).astype(BF16)
        lines = slice(i * STEPS * total, (i + 1) * STEPS * total)
        attn_out[lines, :] = attn
        outs[n // 2][slots * (depth + KEPT) + lines.start : slots * (depth + KEPT) + lines.stop, :] = attn


def project(n, lines, weight, pieces):
    me = lax.axis_index("beam")
    dim = next(iter(pieces.values()))[0].shape[1]
    heads = weight.shape[0] // dim // n
    acc = None
    for x, (ref, first) in pieces.items():
        rows = pl.ds(pl.multiple_of((me ^ x) * heads * dim, dim), heads * dim)
        lhs = [ref[first + i * lines : first + (i + 1) * lines, :] for i in range(heads)]
        term = jnp.dot(jnp.concatenate(lhs, 1), weight[rows, :], preferred_element_type=F32)
        acc = term if acc is None else acc + term
    return acc


def relay_kernel(have, got, out):
    more = out.shape[0] - have.shape[0]
    out[: have.shape[0], :] = have[...]
    out[have.shape[0] :, :] = got[got.shape[0] - more :, :]


def project_kernel(n, order, head_count, weight, begun, *rest):
    keep, send, terms = rest[-3:]
    pieces = {}
    for places, ref in zip(order, rest):
        pieces |= {x: (ref, at * (ref.shape[0] // len(places))) for at, x in enumerate(places)}
    head, lines = lax.axis_index("head"), terms.shape[0]
    terms[...] = begun[...] + project(n, lines, weight, pieces)
    part = lines // STEPS // head_count
    for t in range(STEPS):
        own = pl.multiple_of(t * part * head_count + head * part, part)
        other = pl.multiple_of(t * part * head_count + (1 - head) * part, part)
        keep[t] = terms[pl.ds(own, part), :]
        send[t] = terms[pl.ds(other, part), :]


def final_kernel(n, order, first, decay, k, v, *rest):
    if first:
        weight, attn, *rest = rest
    ins, (result, *terms, out, ks, vs, sem) = dict(zip(order, rest)), rest[-5 - first :]
    slots, dim, columns = result.shape
    if first:
        across = ins[n // 2]
        pieces = {0: (attn, 0), n // 2: (across, across.shape[0] - attn.shape[0])}
        terms[0][...] = project(n, terms[0].shape[0], weight, pieces)
    heads = columns // dim // n
    depth = heads * dim
    me = lax.axis_index("beam")
    ks[...] = k[1].astype(F32)
    vs[...] = v[1].astype(F32)
    line = lax.broadcasted_iota(jnp.int32, (16, dim), 0)
    copies = []
    for x in order:
        extra = ins[x][slots * depth : slots * (depth + KEPT), :].astype(F32)
        for j in range(slots):
            for i in range(heads):
                h = (me ^ x) * heads + i
                d = decay[pl.ds(h, 1), :]
                at = pl.ds(pl.multiple_of(h * dim, dim), dim)
                row = j * KEPT + i * 2
                k1, v1 = extra[row : row + 1], extra[row + 1 : row + 2]
                scaled = d * v1
                high = scaled.astype(BF16).astype(F32)
                low = scaled - high
                lhs = jnp.where(line < 2, k1, jnp.where(line == 2, ks[j : j + 1, at], 0.0))
                rhs = jnp.where(line == 0, high, jnp.where(line == 1, low, vs[j : j + 1, at]))
                outer = lax.dot_general(
                    lhs.astype(BF16), rhs.astype(BF16), (((0,), (0,)), ((), ())), preferred_element_type=F32
                )
                first = j * depth + i * dim
                out[j, :, at] = (d * d) * ins[x][first : first + dim, :].astype(F32) + outer
        at = pl.ds(pl.multiple_of((me ^ x) * depth, depth), depth)
        copies.append(pltpu.make_async_copy(out.at[:, :, at], result.at[:, :, at], sem.at[x]))
        copies[-1].start()
    for c in copies:
        c.wait()


def fast(n, head_count, states, decay_rates, queries, key_vectors, values, gate_logits, parents, out_weight):
    slots, dim, columns = states.shape
    heads = columns // dim // n
    total, depth = n * slots, heads * dim
    first, second = [4, 1, 2, 5, 3, 6, 7, 0], [4, 1, 2, 5, 3, 6, 7, 0]
    decay = jnp.broadcast_to(jnp.exp(-decay_rates)[:, None], (columns // dim, dim))

    def exchange(order, chunks):
        return [
            lax.ppermute(chunk, "beam", [(j, j ^ x) for j in range(n)]) if x else chunk
            for x, chunk in zip(order, chunks)
        ]

    table = jnp.concatenate([parents, parents * EXTRA], 0)
    packed = []
    for part in (first[:1], first[1:]):
        packed += pl.pallas_call(
            functools.partial(pack_kernel, n, part),
            out_shape=[jax.ShapeDtypeStruct((slots, depth + EXTRA, dim), BF16)] * len(part),
            in_specs=[ANY] * 5,
            out_specs=[ANY] * len(part),
            scratch_shapes=[
                pltpu.VMEM((slots, dim, columns), F32),
                pltpu.VMEM((ARRAYS, *queries.shape), BF16),
                pltpu.VMEM((slots, ARRAYS * STEPS, columns), F32),
                pltpu.VMEM((n, slots, depth + EXTRA, dim), BF16),
                pltpu.SemaphoreType.DMA((n,)),
                pltpu.SemaphoreType.DMA((ARRAYS,)),
                pltpu.SemaphoreType.DMA((n,)),
            ],
        )(states, queries, key_vectors, values, gate_logits)
    packed[-1] = pl.pallas_call(
        hold_kernel,
        out_shape=jax.ShapeDtypeStruct(packed[-1].shape, BF16),
        in_specs=[VMEM],
        out_specs=VMEM,
        compiler_params=params(),
    )(packed[-1])
    attn_shape = jax.ShapeDtypeStruct((heads * STEPS * total, dim), BF16)
    lines = slots * (depth + KEPT)
    *picked, attn = pl.pallas_call(
        functools.partial(middle_kernel, n, first, second),
        out_shape=[
            jax.ShapeDtypeStruct((lines + (attn_shape.shape[0] if x == n // 2 else 0), dim), BF16) for x in second
        ]
        + [attn_shape],
        in_specs=[ANY] + [VMEM] * n + [ANY],
        out_specs=[VMEM] * (n + 1),
        scratch_shapes=[
            pltpu.VMEM((heads, total * dim, dim), BF16),
            pltpu.VMEM((total * EXTRA, dim), F32),
            pltpu.VMEM((slots * KEPT, dim), F32),
            pltpu.SMEM(table.shape, jnp.int32),
            pltpu.VMEM((slots, depth + EXTRA, dim), BF16),
            pltpu.SemaphoreType.DMA((2,)),
        ],
        compiler_params=params(),
    )(table, decay, *exchange(first, packed))
    forked = exchange(second, picked)
    held = dict(zip(second, forked))
    have, got, places, hop = attn, held[n // 2], [0, n // 2], 1
    relayed = {}
    while hop < n // 2:
        have = pl.pallas_call(
            relay_kernel,
            out_shape=jax.ShapeDtypeStruct((len(places) * attn.shape[0], dim), BF16),
            in_specs=[VMEM] * 2,
            out_specs=VMEM,
            compiler_params=params(),
        )(have, got)
        (got,) = exchange([hop], [have])
        relayed[tuple(x ^ hop for x in places)] = got
        places += [x ^ hop for x in places]
        hop *= 2

    whole = jax.ShapeDtypeStruct(states.shape, F32)

    def finish(part, *before):
        more = [] if before else [out_weight, attn]
        return pl.pallas_call(
            functools.partial(final_kernel, n, part, not before),
            out_shape=[whole] if before else [whole, jax.ShapeDtypeStruct((STEPS * total, out_weight.shape[1]), F32)],
            in_specs=[VMEM] * (len(more) + len(part) + 3) + [ANY] * len(before),
            out_specs=[ANY] if before else [ANY, VMEM],
            input_output_aliases={len(part) + 3: 0} if before else {},
            scratch_shapes=[
                pltpu.VMEM(states.shape, F32),
                pltpu.VMEM((slots, columns), F32),
                pltpu.VMEM((slots, columns), F32),
                pltpu.SemaphoreType.DMA((n,)),
            ],
            compiler_params=params(),
        )(decay, key_vectors, values, *more, *[held[x] for x in part], *before)

    begun, partial = finish(second[:5] + second[-1:])
    piece = jax.ShapeDtypeStruct((STEPS, total // head_count, out_weight.shape[1]), F32)
    keep, send = pl.pallas_call(
        functools.partial(project_kernel, n, list(relayed), head_count),
        out_shape=[piece, piece],
        in_specs=[VMEM] * (2 + len(relayed)),
        out_specs=[VMEM] * 2,
        scratch_shapes=[pltpu.VMEM((STEPS * total, out_weight.shape[1]), F32)],
        compiler_params=params(),
    )(out_weight, partial, *relayed.values())
    other = lax.ppermute(send, "head", [(0, 1), (1, 0)])
    projected = (keep + other).astype(BF16)
    (final,) = finish(second[5:-1], begun)
    return projected, final


def fork(state, parent_list):
    row_state = lax.all_to_all(state, "beam", split_axis=1, concat_axis=0, tiled=True)
    picked = jnp.take(row_state, parent_list, axis=0)
    return lax.all_to_all(picked, "beam", split_axis=0, concat_axis=1, tiled=True)


def general(states, decay_rates, queries, key_vectors, values, gate_logits, parents, out_weight):
    slot_count, head_dim, columns = states.shape
    groups = columns // head_dim
    decay = jnp.exp(-decay_rates)
    current = states
    readouts = []
    for step in range(parents.shape[0]):
        forked = fork(current, parents[step])
        query_f = queries[step].astype(F32).reshape(slot_count, groups, head_dim)
        key_f = key_vectors[step].astype(F32).reshape(slot_count, groups, head_dim)
        value_f = values[step].astype(F32).reshape(slot_count, groups, head_dim)
        grid = forked.reshape(slot_count, head_dim, groups, head_dim)
        updated = decay[None, None, :, None] * grid + jnp.einsum("shi,shj->sihj", key_f, value_f)
        readout = jnp.einsum("shi,sihj->shj", query_f, updated, precision=lax.Precision.HIGHEST)
        current = updated.reshape(slot_count, head_dim, columns)
        readouts.append(readout.reshape(slot_count, columns))
    stacked = jnp.stack(readouts)
    attn = (jax.nn.sigmoid(gate_logits.astype(F32)) * stacked).astype(BF16)
    terms = jnp.einsum(
        "tsc,cd->tsd",
        lax.all_gather(attn, "beam", axis=1, tiled=True),
        out_weight,
        preferred_element_type=F32,
    )
    projected = lax.psum_scatter(terms, "head", scatter_dimension=1, tiled=True).astype(BF16)
    return (projected, current)


def solution(mesh):
    n, head_count = mesh.shape["beam"], mesh.shape["head"]

    def shards(*args):
        columns, dim = args[0].shape[2], args[0].shape[1]
        if n & (n - 1) == 0 and columns // dim == 2 * n and head_count == 2:
            return fast(n, head_count, *args)
        return general(*args)

    in_specs = (
        P(("parts", "beam"), None, "head"),
        P("head"),
        P(None, ("parts", "beam"), "head"),
        P(None, ("parts", "beam"), "head"),
        P(None, ("parts", "beam"), "head"),
        P(None, ("parts", "beam"), "head"),
        P(None, "parts"),
        P("head", "beam"),
    )
    out_specs = (P(None, ("parts", "head"), "beam"), P(("parts", "beam"), None, "head"))
    return jax.shard_map(shards, mesh=mesh, in_specs=in_specs, out_specs=out_specs, check_vma=False)
```

```python
import functools

import jax
import jax.numpy as jnp
from jax import lax
from jax.experimental import pallas as pl
from jax.experimental.pallas import tpu as pltpu
from jax.sharding import PartitionSpec as P

F32, BF16 = jnp.float32, jnp.bfloat16
VMEM = pl.BlockSpec(memory_space=pltpu.VMEM)
SMEM = pl.BlockSpec(memory_space=pltpu.SMEM)
ANY = pl.BlockSpec(memory_space=pl.ANY)
STEPS, ARRAYS = 2, 4
Q, K, V, G = range(ARRAYS)
EXTRA = 16
KEPT = 8


def params(limit=48):
    return pltpu.CompilerParams(vmem_limit_bytes=limit << 20)


def cost(flops, moved):
    return pl.CostEstimate(flops=flops, bytes_accessed=moved, transcendentals=0)


def row_of(head, array, step):
    return head * ARRAYS * STEPS + array * STEPS + step


def by_partner(order, refs):
    return [ref for _, ref in sorted(zip(order, refs), key=lambda pair: pair[0])]


def pack_kernel(n, order, st_hbm, q, k, v, g, *rest):
    outs, (st, vectors, rows, chunk, sem, sem_small, sem_out) = dict(zip(order, rest)), rest[-7:]
    slots, dim, columns = st.shape
    heads = columns // dim // n
    me = lax.axis_index("beam")

    def lanes(head, count):
        return pl.ds(pl.multiple_of(head * dim, dim), count * dim)

    at = lanes((me ^ order[0]) * heads, heads) if len(order) == 1 else slice(None)
    small = [
        pltpu.make_async_copy(ref.at[:, :, at], vectors.at[a, :, :, at], sem_small.at[a])
        for a, ref in enumerate((q, k, v, g))
    ]
    large = {}
    for x in order:
        here = lanes((me ^ x) * heads, heads)
        large[x] = pltpu.make_async_copy(st_hbm.at[:, :, here], st.at[:, :, here], sem.at[x])
    for c in [large[order[0]], *small, *list(large.values())[1:]]:
        c.start()
    for a in range(ARRAYS):
        small[a].wait()
        whole = vectors[a, :, :, at].astype(F32)
        for t in range(STEPS):
            for j in range(slots):
                rows[j, a * STEPS + t : a * STEPS + t + 1, at] = whole[t, j : j + 1]
    for x in order:
        large[x].wait()
        first = (me ^ x) * heads
        for j in range(slots):
            extra = []
            for i in range(heads):
                at = lanes(first + i, 1)
                chunk[x, j, i * dim : (i + 1) * dim, :] = st[j, :, at].astype(BF16)
                extra.append(rows[j, :, at])
            chunk[x, j, heads * dim :, :] = jnp.concatenate(extra, 0).astype(BF16)
        large[x] = pltpu.make_async_copy(chunk.at[x], outs[x], sem_out.at[x])
        large[x].start()
    for x in order:
        large[x].wait()


def hold_kernel(chunk, out):
    out[...] = chunk[...]


def middle_kernel(n, first, second, parents_hbm, decay, *rest):
    ins, outs = by_partner(first, rest[:n]), by_partner(second, rest[n : 2 * n])
    attn_out, buf, vectors, kept, parents, own, sem = rest[2 * n :]
    copies = [pltpu.make_async_copy(parents_hbm, parents, sem.at[0]), pltpu.make_async_copy(ins[0], own, sem.at[1])]
    for c in copies:
        c.start()
    ins[0] = own
    slots, rows, dim = own.shape
    depth = rows - EXTRA
    heads = depth // dim
    total = n * slots
    me = lax.axis_index("beam")
    for x in [*range(1, n), 0]:
        if x == 0:
            for c in copies:
                c.wait()
        for j in range(slots):
            slot = (me ^ x) * slots + j
            for i in range(heads):
                to = pl.ds(pl.multiple_of(slot * dim, dim), dim)
                buf[i, to, :] = ins[x][j, i * dim : (i + 1) * dim, :]
            at = pl.multiple_of(slot * EXTRA, EXTRA)
            vectors[pl.ds(at, EXTRA), :] = ins[x][j, depth:, :].astype(F32)
    for x in range(n):
        for j in range(slots):
            middle = parents[1, (me ^ x) * slots + j]
            root = pl.ds(pl.multiple_of(parents[0, middle] * dim, dim), dim)
            for i in range(heads):
                outs[x][j * depth + i * dim : j * depth + (i + 1) * dim, :] = buf[i, root, :]
            for i in range(heads):
                for place, array in enumerate((K, V)):
                    to = j * KEPT + i * 2 + place
                    kept[to : to + 1, :] = vectors[pl.ds(parents[STEPS + 1, (me ^ x) * slots + j] + row_of(i, array, 0), 1), :]
        outs[x][slots * depth : slots * (depth + KEPT), :] = kept[...].astype(BF16)
    line = lax.broadcasted_iota(jnp.int32, (STEPS * total, dim), 0)
    mid_line = lax.broadcasted_iota(jnp.int32, (total, total), 0)
    source = jnp.zeros((STEPS * total, dim), jnp.int32)
    chosen = jnp.zeros((total, total), jnp.int32)
    for c in range(total):
        middle = parents[1, c]
        source = jnp.where(line == c, parents[0, c], source)
        source = jnp.where(line == total + c, parents[0, middle], source)
        chosen = jnp.where(mid_line == c, middle, chosen)
    pick = (chosen == lax.broadcasted_iota(jnp.int32, (total, total), 1)).astype(BF16)
    for i in range(heads):
        d = decay[pl.ds(me * heads + i, 1), :]

        def get(array, step):
            return vectors[pl.ds(row_of(i, array, step), total, stride=EXTRA), :]

        q1, q2, k1, k2 = get(Q, 0), get(Q, 1), get(K, 0), get(K, 1)
        v1, v2 = get(V, 0), get(V, 1)
        queries = jnp.concatenate([q1, q2], 0)
        mine = [jnp.where(source == slot, queries, 0.0).astype(BF16) for slot in range(total)]
        acc = jnp.dot(jnp.concatenate(mine, 1), buf[i], preferred_element_type=F32)
        k1m = jnp.dot(pick, k1.astype(BF16), preferred_element_type=F32)
        v1m = jnp.dot(pick, v1.astype(BF16), preferred_element_type=F32)
        r1 = d * acc[:total] + jnp.sum(q1 * k1, -1, keepdims=True) * v1
        r2 = d * (d * acc[total:] + jnp.sum(q2 * k1m, -1, keepdims=True) * v1m)
        r2 = r2 + jnp.sum(q2 * k2, -1, keepdims=True) * v2
        attn = [jax.nn.sigmoid(get(G, 0)) * r1, jax.nn.sigmoid(get(G, 1)) * r2]
        attn = jnp.concatenate(attn, 0).astype(BF16)
        lines = slice(i * STEPS * total, (i + 1) * STEPS * total)
        attn_out[lines, :] = attn
        outs[n // 2][slots * (depth + KEPT) + lines.start : slots * (depth + KEPT) + lines.stop, :] = attn


def project(n, lines, weight, pieces):
    me = lax.axis_index("beam")
    dim = next(iter(pieces.values()))[0].shape[1]
    heads = weight.shape[0] // dim // n
    acc = None
    for x, (ref, first) in pieces.items():
        rows = pl.ds(pl.multiple_of((me ^ x) * heads * dim, dim), heads * dim)
        lhs = [ref[first + i * lines : first + (i + 1) * lines, :] for i in range(heads)]
        term = jnp.dot(jnp.concatenate(lhs, 1), weight[rows, :], preferred_element_type=F32)
        acc = term if acc is None else acc + term
    return acc


def relay_kernel(have, got, out):
    more = out.shape[0] - have.shape[0]
    out[: have.shape[0], :] = have[...]
    out[have.shape[0] :, :] = got[got.shape[0] - more :, :]


def project_kernel(n, order, head_count, weight, begun, *rest):
    keep, send, terms = rest[-3:]
    pieces = {}
    for places, ref in zip(order, rest):
        pieces |= {x: (ref, at * (ref.shape[0] // len(places))) for at, x in enumerate(places)}
    head, lines = lax.axis_index("head"), terms.shape[0]
    terms[...] = begun[...] + project(n, lines, weight, pieces)
    part = lines // STEPS // head_count
    for t in range(STEPS):
        own = pl.multiple_of(t * part * head_count + head * part, part)
        other = pl.multiple_of(t * part * head_count + (1 - head) * part, part)
        keep[t] = terms[pl.ds(own, part), :]
        send[t] = terms[pl.ds(other, part), :]


def final_kernel(n, order, first, decay, k, v, *rest):
    if first:
        weight, attn, *rest = rest
    ins, (result, *more, out, ks, vs, total, sem) = dict(zip(order, rest)), rest[-7:]
    if first:
        terms = more
    else:
        keep, other = rest[len(order) + 1 : len(order) + 3]
        total[...] = (keep[...] + other[...]).astype(BF16)
        projected = pltpu.make_async_copy(total, more[0], sem.at[n])
        projected.start()
    slots, dim, columns = result.shape
    if first:
        across = ins[n // 2]
        pieces = {0: (attn, 0), n // 2: (across, across.shape[0] - attn.shape[0])}
        terms[0][...] = project(n, terms[0].shape[0], weight, pieces)
    heads = columns // dim // n
    depth = heads * dim
    me = lax.axis_index("beam")
    ks[...] = k[1].astype(F32)
    vs[...] = v[1].astype(F32)
    line = lax.broadcasted_iota(jnp.int32, (16, dim), 0)
    copies = []
    for x in order:
        extra = ins[x][slots * depth : slots * (depth + KEPT), :].astype(F32)
        for j in range(slots):
            for i in range(heads):
                h = (me ^ x) * heads + i
                d = decay[pl.ds(h, 1), :]
                at = pl.ds(pl.multiple_of(h * dim, dim), dim)
                row = j * KEPT + i * 2
                k1, v1 = extra[row : row + 1], extra[row + 1 : row + 2]
                scaled = d * v1
                high = scaled.astype(BF16).astype(F32)
                low = scaled - high
                lhs = jnp.where(line < 2, k1, jnp.where(line == 2, ks[j : j + 1, at], 0.0))
                rhs = jnp.where(line == 0, high, jnp.where(line == 1, low, vs[j : j + 1, at]))
                outer = lax.dot_general(
                    lhs.astype(BF16), rhs.astype(BF16), (((0,), (0,)), ((), ())), preferred_element_type=F32
                )
                begin = j * depth + i * dim
                out[j, :, at] = (d * d) * ins[x][begin : begin + dim, :].astype(F32) + outer
        at = pl.ds(pl.multiple_of((me ^ x) * depth, depth), depth)
        copies.append(pltpu.make_async_copy(out.at[:, :, at], result.at[:, :, at], sem.at[x]))
        copies[-1].start()
    for c in copies:
        c.wait()
    if not first:
        projected.wait()


def fast(n, head_count, states, decay_rates, queries, key_vectors, values, gate_logits, parents, out_weight):
    slots, dim, columns = states.shape
    heads = columns // dim // n
    total, depth = n * slots, heads * dim
    first, second = [4, 1, 2, 3, 5, 6, 7, 0], [4, 1, 2, 5, 3, 6, 7, 0]
    decay = jnp.broadcast_to(jnp.exp(-decay_rates)[:, None], (columns // dim, dim))

    def exchange(order, chunks):
        return [
            lax.ppermute(chunk, "beam", [(j, j ^ x) for j in range(n)]) if x else chunk
            for x, chunk in zip(order, chunks)
        ]

    table = jnp.concatenate([parents, parents * EXTRA], 0)
    packed = []
    for part in (first[:1], first[1:]):
        packed += pl.pallas_call(
            functools.partial(pack_kernel, n, part),
            out_shape=[jax.ShapeDtypeStruct((slots, depth + EXTRA, dim), BF16)] * len(part),
            in_specs=[ANY] * 5,
            out_specs=[ANY] * len(part),
            scratch_shapes=[
                pltpu.VMEM((slots, dim, columns), F32),
                pltpu.VMEM((ARRAYS, *queries.shape), BF16),
                pltpu.VMEM((slots, ARRAYS * STEPS, columns), F32),
                pltpu.VMEM((n, slots, depth + EXTRA, dim), BF16),
                pltpu.SemaphoreType.DMA((n,)),
                pltpu.SemaphoreType.DMA((ARRAYS,)),
                pltpu.SemaphoreType.DMA((n,)),
            ],
        )(states, queries, key_vectors, values, gate_logits)
    packed[-1] = pl.pallas_call(
        hold_kernel,
        out_shape=jax.ShapeDtypeStruct(packed[-1].shape, BF16),
        in_specs=[VMEM],
        out_specs=VMEM,
        compiler_params=params(),
    )(packed[-1])
    attn_shape = jax.ShapeDtypeStruct((heads * STEPS * total, dim), BF16)
    lines = slots * (depth + KEPT)
    *picked, attn = pl.pallas_call(
        functools.partial(middle_kernel, n, first, second),
        out_shape=[
            jax.ShapeDtypeStruct((lines + (attn_shape.shape[0] if x == n // 2 else 0), dim), BF16) for x in second
        ]
        + [attn_shape],
        in_specs=[ANY] + [VMEM] * n + [ANY],
        out_specs=[VMEM] * (n + 1),
        scratch_shapes=[
            pltpu.VMEM((heads, total * dim, dim), BF16),
            pltpu.VMEM((total * EXTRA, dim), F32),
            pltpu.VMEM((slots * KEPT, dim), F32),
            pltpu.SMEM(table.shape, jnp.int32),
            pltpu.VMEM((slots, depth + EXTRA, dim), BF16),
            pltpu.SemaphoreType.DMA((2,)),
        ],
        compiler_params=params(),
    )(table, decay, *exchange(first, packed))
    forked = exchange(second, picked)
    held = dict(zip(second, forked))
    have, got, places, hop = attn, held[n // 2], [0, n // 2], 1
    relayed = {}
    while hop < n // 2:
        have = pl.pallas_call(
            relay_kernel,
            out_shape=jax.ShapeDtypeStruct((len(places) * attn.shape[0], dim), BF16),
            in_specs=[VMEM] * 2,
            out_specs=VMEM,
            compiler_params=params(),
        )(have, got)
        (got,) = exchange([hop], [have])
        relayed[tuple(x ^ hop for x in places)] = got
        places += [x ^ hop for x in places]
        hop *= 2

    whole = jax.ShapeDtypeStruct(states.shape, F32)
    summed = jax.ShapeDtypeStruct((STEPS, total // head_count, out_weight.shape[1]), BF16)

    def finish(part, *before):
        more = [] if before else [out_weight, attn]
        return pl.pallas_call(
            functools.partial(final_kernel, n, part, not before),
            out_shape=[whole, summed if before else jax.ShapeDtypeStruct((STEPS * total, out_weight.shape[1]), F32)],
            in_specs=[VMEM] * (len(more) + len(part) + 3) + ([ANY, VMEM, VMEM] if before else []),
            out_specs=[ANY, ANY if before else VMEM],
            input_output_aliases={len(part) + 3: 0} if before else {},
            scratch_shapes=[
                pltpu.VMEM(states.shape, F32),
                pltpu.VMEM((slots, columns), F32),
                pltpu.VMEM((slots, columns), F32),
                pltpu.VMEM(summed.shape, BF16),
                pltpu.SemaphoreType.DMA((n + 1,)),
            ],
            compiler_params=params(),
        )(decay, key_vectors, values, *more, *[held[x] for x in part], *before)

    begun, partial = finish(second[:5] + second[-1:])
    piece = jax.ShapeDtypeStruct((STEPS, total // head_count, out_weight.shape[1]), F32)
    keep, send = pl.pallas_call(
        functools.partial(project_kernel, n, list(relayed), head_count),
        out_shape=[piece, piece],
        in_specs=[VMEM] * (2 + len(relayed)),
        out_specs=[VMEM] * 2,
        scratch_shapes=[pltpu.VMEM((STEPS * total, out_weight.shape[1]), F32)],
        compiler_params=params(),
    )(out_weight, partial, *relayed.values())
    other = lax.ppermute(send, "head", [(0, 1), (1, 0)])
    final, projected = finish(second[5:-1], begun, keep, other)
    return projected, final


def fork(state, parent_list):
    row_state = lax.all_to_all(state, "beam", split_axis=1, concat_axis=0, tiled=True)
    picked = jnp.take(row_state, parent_list, axis=0)
    return lax.all_to_all(picked, "beam", split_axis=0, concat_axis=1, tiled=True)


def general(states, decay_rates, queries, key_vectors, values, gate_logits, parents, out_weight):
    slot_count, head_dim, columns = states.shape
    groups = columns // head_dim
    decay = jnp.exp(-decay_rates)
    current = states
    readouts = []
    for step in range(parents.shape[0]):
        forked = fork(current, parents[step])
        query_f = queries[step].astype(F32).reshape(slot_count, groups, head_dim)
        key_f = key_vectors[step].astype(F32).reshape(slot_count, groups, head_dim)
        value_f = values[step].astype(F32).reshape(slot_count, groups, head_dim)
        grid = forked.reshape(slot_count, head_dim, groups, head_dim)
        updated = decay[None, None, :, None] * grid + jnp.einsum("shi,shj->sihj", key_f, value_f)
        readout = jnp.einsum("shi,sihj->shj", query_f, updated, precision=lax.Precision.HIGHEST)
        current = updated.reshape(slot_count, head_dim, columns)
        readouts.append(readout.reshape(slot_count, columns))
    stacked = jnp.stack(readouts)
    attn = (jax.nn.sigmoid(gate_logits.astype(F32)) * stacked).astype(BF16)
    terms = jnp.einsum(
        "tsc,cd->tsd",
        lax.all_gather(attn, "beam", axis=1, tiled=True),
        out_weight,
        preferred_element_type=F32,
    )
    projected = lax.psum_scatter(terms, "head", scatter_dimension=1, tiled=True).astype(BF16)
    return (projected, current)


def solution(mesh):
    n, head_count = mesh.shape["beam"], mesh.shape["head"]

    def shards(*args):
        columns, dim = args[0].shape[2], args[0].shape[1]
        if n & (n - 1) == 0 and columns // dim == 2 * n and head_count == 2:
            return fast(n, head_count, *args)
        return general(*args)

    in_specs = (
        P(("parts", "beam"), None, "head"),
        P("head"),
        P(None, ("parts", "beam"), "head"),
        P(None, ("parts", "beam"), "head"),
        P(None, ("parts", "beam"), "head"),
        P(None, ("parts", "beam"), "head"),
        P(None, "parts"),
        P("head", "beam"),
    )
    out_specs = (P(None, ("parts", "head"), "beam"), P(("parts", "beam"), None, "head"))
    return jax.shard_map(shards, mesh=mesh, in_specs=in_specs, out_specs=out_specs, check_vma=False)
```

```python
import functools

import jax
import jax.numpy as jnp
from jax import lax
from jax.experimental import pallas as pl
from jax.experimental.pallas import tpu as pltpu
from jax.sharding import PartitionSpec as P

F32, BF16 = jnp.float32, jnp.bfloat16
VMEM = pl.BlockSpec(memory_space=pltpu.VMEM)
SMEM = pl.BlockSpec(memory_space=pltpu.SMEM)
ANY = pl.BlockSpec(memory_space=pl.ANY)
STEPS, ARRAYS = 2, 4
Q, K, V, G = range(ARRAYS)
EXTRA = 16
KEPT = 8


def params(limit=48):
    return pltpu.CompilerParams(vmem_limit_bytes=limit << 20)


def cost(flops, moved):
    return pl.CostEstimate(flops=flops, bytes_accessed=moved, transcendentals=0)


def row_of(head, array, step):
    return head * ARRAYS * STEPS + array * STEPS + step


def by_partner(order, refs):
    return [ref for _, ref in sorted(zip(order, refs), key=lambda pair: pair[0])]


def pack_kernel(n, order, st_hbm, q, k, v, g, *rest):
    outs, (st, vectors, rows, chunk, sem, sem_small, sem_out) = dict(zip(order, rest)), rest[-7:]
    slots, dim, columns = st.shape
    heads = columns // dim // n
    me = lax.axis_index("beam")

    def lanes(head, count):
        return pl.ds(pl.multiple_of(head * dim, dim), count * dim)

    at = lanes((me ^ order[0]) * heads, heads) if len(order) == 1 else slice(None)
    small = [
        pltpu.make_async_copy(ref.at[:, :, at], vectors.at[a, :, :, at], sem_small.at[a])
        for a, ref in enumerate((q, k, v, g))
    ]
    large = {}
    for x in order:
        here = lanes((me ^ x) * heads, heads)
        large[x] = pltpu.make_async_copy(st_hbm.at[:, :, here], st.at[:, :, here], sem.at[x])
    for c in [large[order[0]], *small, *list(large.values())[1:]]:
        c.start()
    for a in range(ARRAYS):
        small[a].wait()
        whole = vectors[a, :, :, at].astype(F32)
        for t in range(STEPS):
            for j in range(slots):
                rows[j, a * STEPS + t : a * STEPS + t + 1, at] = whole[t, j : j + 1]
    for x in order:
        large[x].wait()
        first = (me ^ x) * heads
        for j in range(slots):
            extra = []
            for i in range(heads):
                at = lanes(first + i, 1)
                chunk[x, j, i * dim : (i + 1) * dim, :] = st[j, :, at].astype(BF16)
                extra.append(rows[j, :, at])
            chunk[x, j, heads * dim :, :] = jnp.concatenate(extra, 0).astype(BF16)
        large[x] = pltpu.make_async_copy(chunk.at[x], outs[x], sem_out.at[x])
        large[x].start()
    for x in order:
        large[x].wait()


def hold_kernel(chunk, out):
    out[...] = chunk[...]


def middle_kernel(n, first, second, parents_hbm, decay, *rest):
    ins, outs = by_partner(first, rest[:n]), by_partner(second, rest[n : 2 * n])
    attn_out, buf, vectors, kept, parents, own, sem = rest[2 * n :]
    copies = [pltpu.make_async_copy(parents_hbm, parents, sem.at[0]), pltpu.make_async_copy(ins[0], own, sem.at[1])]
    for c in copies:
        c.start()
    ins[0] = own
    slots, rows, dim = own.shape
    depth = rows - EXTRA
    heads = depth // dim
    total = n * slots
    me = lax.axis_index("beam")
    for x in [*range(1, n), 0]:
        if x == 0:
            for c in copies:
                c.wait()
        for j in range(slots):
            slot = (me ^ x) * slots + j
            for i in range(heads):
                to = pl.ds(pl.multiple_of(slot * dim, dim), dim)
                buf[i, to, :] = ins[x][j, i * dim : (i + 1) * dim, :]
            at = pl.multiple_of(slot * EXTRA, EXTRA)
            vectors[pl.ds(at, EXTRA), :] = ins[x][j, depth:, :].astype(F32)
    for x in range(n):
        for j in range(slots):
            middle = parents[1, (me ^ x) * slots + j]
            root = pl.ds(pl.multiple_of(parents[0, middle] * dim, dim), dim)
            for i in range(heads):
                outs[x][j * depth + i * dim : j * depth + (i + 1) * dim, :] = buf[i, root, :]
            for i in range(heads):
                for place, array in enumerate((K, V)):
                    to = j * KEPT + i * 2 + place
                    kept[to : to + 1, :] = vectors[pl.ds(parents[STEPS + 1, (me ^ x) * slots + j] + row_of(i, array, 0), 1), :]
        outs[x][slots * depth : slots * (depth + KEPT), :] = kept[...].astype(BF16)
    line = lax.broadcasted_iota(jnp.int32, (STEPS * total, dim), 0)
    mid_line = lax.broadcasted_iota(jnp.int32, (total, total), 0)
    source = jnp.zeros((STEPS * total, dim), jnp.int32)
    chosen = jnp.zeros((total, total), jnp.int32)
    for c in range(total):
        middle = parents[1, c]
        source = jnp.where(line == c, parents[0, c], source)
        source = jnp.where(line == total + c, parents[0, middle], source)
        chosen = jnp.where(mid_line == c, middle, chosen)
    pick = (chosen == lax.broadcasted_iota(jnp.int32, (total, total), 1)).astype(BF16)
    for i in range(heads):
        d = decay[pl.ds(me * heads + i, 1), :]

        def get(array, step):
            return vectors[pl.ds(row_of(i, array, step), total, stride=EXTRA), :]

        q1, q2, k1, k2 = get(Q, 0), get(Q, 1), get(K, 0), get(K, 1)
        v1, v2 = get(V, 0), get(V, 1)
        queries = jnp.concatenate([q1, q2], 0)
        mine = [jnp.where(source == slot, queries, 0.0).astype(BF16) for slot in range(total)]
        acc = jnp.dot(jnp.concatenate(mine, 1), buf[i], preferred_element_type=F32)
        k1m = jnp.dot(pick, k1.astype(BF16), preferred_element_type=F32)
        v1m = jnp.dot(pick, v1.astype(BF16), preferred_element_type=F32)
        r1 = d * acc[:total] + jnp.sum(q1 * k1, -1, keepdims=True) * v1
        r2 = d * (d * acc[total:] + jnp.sum(q2 * k1m, -1, keepdims=True) * v1m)
        r2 = r2 + jnp.sum(q2 * k2, -1, keepdims=True) * v2
        attn = [jax.nn.sigmoid(get(G, 0)) * r1, jax.nn.sigmoid(get(G, 1)) * r2]
        attn = jnp.concatenate(attn, 0).astype(BF16)
        lines = slice(i * STEPS * total, (i + 1) * STEPS * total)
        attn_out[lines, :] = attn
        outs[n // 2][slots * (depth + KEPT) + lines.start : slots * (depth + KEPT) + lines.stop, :] = attn


def project(n, lines, weight, pieces):
    me = lax.axis_index("beam")
    dim = next(iter(pieces.values()))[0].shape[1]
    heads = weight.shape[0] // dim // n
    acc = None
    for x, (ref, first) in pieces.items():
        rows = pl.ds(pl.multiple_of((me ^ x) * heads * dim, dim), heads * dim)
        lhs = [ref[first + i * lines : first + (i + 1) * lines, :] for i in range(heads)]
        term = jnp.dot(jnp.concatenate(lhs, 1), weight[rows, :], preferred_element_type=F32)
        acc = term if acc is None else acc + term
    return acc


def relay_kernel(have, got, out):
    more = out.shape[0] - have.shape[0]
    out[: have.shape[0], :] = have[...]
    out[have.shape[0] :, :] = got[got.shape[0] - more :, :]


def project_kernel(n, order, head_count, weight, begun, *rest):
    keep, send, terms = rest[-3:]
    pieces = {}
    for places, ref in zip(order, rest):
        pieces |= {x: (ref, at * (ref.shape[0] // len(places))) for at, x in enumerate(places)}
    head, lines = lax.axis_index("head"), terms.shape[0]
    terms[...] = begun[...] + project(n, lines, weight, pieces)
    part = lines // STEPS // head_count
    for t in range(STEPS):
        own = pl.multiple_of(t * part * head_count + head * part, part)
        other = pl.multiple_of(t * part * head_count + (1 - head) * part, part)
        keep[t] = terms[pl.ds(own, part), :]
        send[t] = terms[pl.ds(other, part), :]


def final_kernel(n, order, first, decay, k, v, *rest):
    if first:
        weight, attn, *rest = rest
    ins, (result, *more, out, ks, vs, total, sem) = dict(zip(order, rest)), rest[-7:]
    if first:
        terms = more
    else:
        keep, other = rest[len(order) + 1 : len(order) + 3]
        total[...] = (keep[...] + other[...]).astype(BF16)
        projected = pltpu.make_async_copy(total, more[0], sem.at[n])
        projected.start()
    slots, dim, columns = result.shape
    if first:
        across = ins[n // 2]
        pieces = {0: (attn, 0), n // 2: (across, across.shape[0] - attn.shape[0])}
        terms[0][...] = project(n, terms[0].shape[0], weight, pieces)
    heads = columns // dim // n
    depth = heads * dim
    me = lax.axis_index("beam")
    ks[...] = k[1].astype(F32)
    vs[...] = v[1].astype(F32)
    line = lax.broadcasted_iota(jnp.int32, (16, dim), 0)
    copies = []
    for x in order:
        extra = ins[x][slots * depth : slots * (depth + KEPT), :].astype(F32)
        for j in range(slots):
            for i in range(heads):
                h = (me ^ x) * heads + i
                d = decay[pl.ds(h, 1), :]
                at = pl.ds(pl.multiple_of(h * dim, dim), dim)
                row = j * KEPT + i * 2
                k1, v1 = extra[row : row + 1], extra[row + 1 : row + 2]
                scaled = d * v1
                high = scaled.astype(BF16).astype(F32)
                low = scaled - high
                lhs = jnp.where(line < 2, k1, jnp.where(line == 2, ks[j : j + 1, at], 0.0))
                rhs = jnp.where(line == 0, high, jnp.where(line == 1, low, vs[j : j + 1, at]))
                outer = lax.dot_general(
                    lhs.astype(BF16), rhs.astype(BF16), (((0,), (0,)), ((), ())), preferred_element_type=F32
                )
                begin = j * depth + i * dim
                out[j, :, at] = (d * d) * ins[x][begin : begin + dim, :].astype(F32) + outer
        at = pl.ds(pl.multiple_of((me ^ x) * depth, depth), depth)
        copies.append(pltpu.make_async_copy(out.at[:, :, at], result.at[:, :, at], sem.at[x]))
        copies[-1].start()
    for c in copies:
        c.wait()
    if not first:
        projected.wait()


def fast(n, head_count, states, decay_rates, queries, key_vectors, values, gate_logits, parents, out_weight):
    slots, dim, columns = states.shape
    heads = columns // dim // n
    total, depth = n * slots, heads * dim
    first, second = [4, 1, 2, 3, 5, 6, 7, 0], [4, 1, 2, 3, 5, 6, 7, 0]
    decay = jnp.broadcast_to(jnp.exp(-decay_rates)[:, None], (columns // dim, dim))

    def exchange(order, chunks):
        return [
            lax.ppermute(chunk, "beam", [(j, j ^ x) for j in range(n)]) if x else chunk
            for x, chunk in zip(order, chunks)
        ]

    table = jnp.concatenate([parents, parents * EXTRA], 0)
    packed = []
    for part in (first[:1], first[1:]):
        packed += pl.pallas_call(
            functools.partial(pack_kernel, n, part),
            out_shape=[jax.ShapeDtypeStruct((slots, depth + EXTRA, dim), BF16)] * len(part),
            in_specs=[ANY] * 5,
            out_specs=[ANY] * len(part),
            scratch_shapes=[
                pltpu.VMEM((slots, dim, columns), F32),
                pltpu.VMEM((ARRAYS, *queries.shape), BF16),
                pltpu.VMEM((slots, ARRAYS * STEPS, columns), F32),
                pltpu.VMEM((n, slots, depth + EXTRA, dim), BF16),
                pltpu.SemaphoreType.DMA((n,)),
                pltpu.SemaphoreType.DMA((ARRAYS,)),
                pltpu.SemaphoreType.DMA((n,)),
            ],
        )(states, queries, key_vectors, values, gate_logits)
    packed[-1] = pl.pallas_call(
        hold_kernel,
        out_shape=jax.ShapeDtypeStruct(packed[-1].shape, BF16),
        in_specs=[VMEM],
        out_specs=VMEM,
        compiler_params=params(),
    )(packed[-1])
    attn_shape = jax.ShapeDtypeStruct((heads * STEPS * total, dim), BF16)
    lines = slots * (depth + KEPT)
    *picked, attn = pl.pallas_call(
        functools.partial(middle_kernel, n, first, second),
        out_shape=[
            jax.ShapeDtypeStruct((lines + (attn_shape.shape[0] if x == n // 2 else 0), dim), BF16) for x in second
        ]
        + [attn_shape],
        in_specs=[ANY] + [VMEM] * n + [ANY],
        out_specs=[VMEM] * (n + 1),
        scratch_shapes=[
            pltpu.VMEM((heads, total * dim, dim), BF16),
            pltpu.VMEM(((total + 1) * EXTRA, dim), F32),
            pltpu.VMEM((slots * KEPT, dim), F32),
            pltpu.SMEM(table.shape, jnp.int32),
            pltpu.VMEM((slots, depth + EXTRA, dim), BF16),
            pltpu.SemaphoreType.DMA((2,)),
        ],
        compiler_params=params(),
    )(table, decay, *exchange(first, packed))
    forked = exchange(second, picked)
    held = dict(zip(second, forked))
    have, got, places, hop = attn, held[n // 2], [0, n // 2], 1
    relayed = {}
    while hop < n // 2:
        have = pl.pallas_call(
            relay_kernel,
            out_shape=jax.ShapeDtypeStruct((len(places) * attn.shape[0], dim), BF16),
            in_specs=[VMEM] * 2,
            out_specs=VMEM,
            compiler_params=params(),
        )(have, got)
        (got,) = exchange([hop], [have])
        relayed[tuple(x ^ hop for x in places)] = got
        places += [x ^ hop for x in places]
        hop *= 2

    whole = jax.ShapeDtypeStruct(states.shape, F32)
    summed = jax.ShapeDtypeStruct((STEPS, total // head_count, out_weight.shape[1]), BF16)

    def finish(part, *before):
        more = [] if before else [out_weight, attn]
        return pl.pallas_call(
            functools.partial(final_kernel, n, part, not before),
            out_shape=[whole, summed if before else jax.ShapeDtypeStruct((STEPS * total, out_weight.shape[1]), F32)],
            in_specs=[VMEM] * (len(more) + len(part) + 3) + ([ANY, VMEM, VMEM] if before else []),
            out_specs=[ANY, ANY if before else VMEM],
            input_output_aliases={len(part) + 3: 0} if before else {},
            scratch_shapes=[
                pltpu.VMEM(states.shape, F32),
                pltpu.VMEM((slots, columns), F32),
                pltpu.VMEM((slots, columns), F32),
                pltpu.VMEM(summed.shape, BF16),
                pltpu.SemaphoreType.DMA((n + 1,)),
            ],
            compiler_params=params(),
        )(decay, key_vectors, values, *more, *[held[x] for x in part], *before)

    begun, partial = finish(second[:5] + second[-1:])
    piece = jax.ShapeDtypeStruct((STEPS, total // head_count, out_weight.shape[1]), F32)
    keep, send = pl.pallas_call(
        functools.partial(project_kernel, n, list(relayed), head_count),
        out_shape=[piece, piece],
        in_specs=[VMEM] * (2 + len(relayed)),
        out_specs=[VMEM] * 2,
        scratch_shapes=[pltpu.VMEM((STEPS * total, out_weight.shape[1]), F32)],
        compiler_params=params(),
    )(out_weight, partial, *relayed.values())
    other = lax.ppermute(send, "head", [(0, 1), (1, 0)])
    final, projected = finish(second[5:-1], begun, keep, other)
    return projected, final


def fork(state, parent_list):
    row_state = lax.all_to_all(state, "beam", split_axis=1, concat_axis=0, tiled=True)
    picked = jnp.take(row_state, parent_list, axis=0)
    return lax.all_to_all(picked, "beam", split_axis=0, concat_axis=1, tiled=True)


def general(states, decay_rates, queries, key_vectors, values, gate_logits, parents, out_weight):
    slot_count, head_dim, columns = states.shape
    groups = columns // head_dim
    decay = jnp.exp(-decay_rates)
    current = states
    readouts = []
    for step in range(parents.shape[0]):
        forked = fork(current, parents[step])
        query_f = queries[step].astype(F32).reshape(slot_count, groups, head_dim)
        key_f = key_vectors[step].astype(F32).reshape(slot_count, groups, head_dim)
        value_f = values[step].astype(F32).reshape(slot_count, groups, head_dim)
        grid = forked.reshape(slot_count, head_dim, groups, head_dim)
        updated = decay[None, None, :, None] * grid + jnp.einsum("shi,shj->sihj", key_f, value_f)
        readout = jnp.einsum("shi,sihj->shj", query_f, updated, precision=lax.Precision.HIGHEST)
        current = updated.reshape(slot_count, head_dim, columns)
        readouts.append(readout.reshape(slot_count, columns))
    stacked = jnp.stack(readouts)
    attn = (jax.nn.sigmoid(gate_logits.astype(F32)) * stacked).astype(BF16)
    terms = jnp.einsum(
        "tsc,cd->tsd",
        lax.all_gather(attn, "beam", axis=1, tiled=True),
        out_weight,
        preferred_element_type=F32,
    )
    projected = lax.psum_scatter(terms, "head", scatter_dimension=1, tiled=True).astype(BF16)
    return (projected, current)


def solution(mesh):
    n, head_count = mesh.shape["beam"], mesh.shape["head"]

    def shards(*args):
        columns, dim = args[0].shape[2], args[0].shape[1]
        if n & (n - 1) == 0 and columns // dim == 2 * n and head_count == 2:
            return fast(n, head_count, *args)
        return general(*args)

    in_specs = (
        P(("parts", "beam"), None, "head"),
        P("head"),
        P(None, ("parts", "beam"), "head"),
        P(None, ("parts", "beam"), "head"),
        P(None, ("parts", "beam"), "head"),
        P(None, ("parts", "beam"), "head"),
        P(None, "parts"),
        P("head", "beam"),
    )
    out_specs = (P(None, ("parts", "head"), "beam"), P(("parts", "beam"), None, "head"))
    return jax.shard_map(shards, mesh=mesh, in_specs=in_specs, out_specs=out_specs, check_vma=False)
```

```python
import functools

import jax
import jax.numpy as jnp
from jax import lax
from jax.experimental import pallas as pl
from jax.experimental.pallas import tpu as pltpu
from jax.sharding import PartitionSpec as P

F32, BF16 = jnp.float32, jnp.bfloat16
VMEM = pl.BlockSpec(memory_space=pltpu.VMEM)
SMEM = pl.BlockSpec(memory_space=pltpu.SMEM)
ANY = pl.BlockSpec(memory_space=pl.ANY)
STEPS, ARRAYS = 2, 4
Q, K, V, G = range(ARRAYS)
EXTRA = 16
KEPT = 8


def params(limit=16):
    return pltpu.CompilerParams(vmem_limit_bytes=limit << 20)


def cost(flops, moved):
    return pl.CostEstimate(flops=flops, bytes_accessed=moved, transcendentals=0)


def row_of(head, array, step):
    return head * ARRAYS * STEPS + array * STEPS + step


def by_partner(order, refs):
    return [ref for _, ref in sorted(zip(order, refs), key=lambda pair: pair[0])]


def pack_kernel(n, order, st_hbm, q, k, v, g, *rest):
    outs, (st, vectors, rows, chunk, sem, sem_small, sem_out) = dict(zip(order, rest)), rest[-7:]
    slots, dim, columns = st.shape
    heads = columns // dim // n
    me = lax.axis_index("beam")

    def lanes(head, count):
        return pl.ds(pl.multiple_of(head * dim, dim), count * dim)

    at = lanes((me ^ order[0]) * heads, heads) if len(order) == 1 else slice(None)
    small = [
        pltpu.make_async_copy(ref.at[:, :, at], vectors.at[a, :, :, at], sem_small.at[a])
        for a, ref in enumerate((q, k, v, g))
    ]
    large = {}
    for x in order:
        here = lanes((me ^ x) * heads, heads)
        large[x] = pltpu.make_async_copy(st_hbm.at[:, :, here], st.at[:, :, here], sem.at[x])
    for c in [large[order[0]], *small, *list(large.values())[1:]]:
        c.start()
    for a in range(ARRAYS):
        small[a].wait()
        whole = vectors[a, :, :, at].astype(F32)
        for t in range(STEPS):
            for j in range(slots):
                rows[j, a * STEPS + t : a * STEPS + t + 1, at] = whole[t, j : j + 1]
    for x in order:
        large[x].wait()
        first = (me ^ x) * heads
        for j in range(slots):
            extra = []
            for i in range(heads):
                at = lanes(first + i, 1)
                chunk[x, j, i * dim : (i + 1) * dim, :] = st[j, :, at].astype(BF16)
                extra.append(rows[j, :, at])
            chunk[x, j, heads * dim :, :] = jnp.concatenate(extra, 0).astype(BF16)
        large[x] = pltpu.make_async_copy(chunk.at[x], outs[x], sem_out.at[x])
        large[x].start()
    for x in order:
        large[x].wait()


def hold_kernel(chunk, out):
    out[...] = chunk[...]


def middle_kernel(n, first, second, parents_hbm, decay, *rest):
    ins, outs = by_partner(first, rest[:n]), by_partner(second, rest[n : 2 * n])
    attn_out, buf, vectors, kept, parents, own, sem = rest[2 * n :]
    copies = [pltpu.make_async_copy(parents_hbm, parents, sem.at[0]), pltpu.make_async_copy(ins[0], own, sem.at[1])]
    for c in copies:
        c.start()
    ins[0] = own
    slots, rows, dim = own.shape
    depth = rows - EXTRA
    heads = depth // dim
    total = n * slots
    me = lax.axis_index("beam")
    for x in [*range(1, n), 0]:
        if x == 0:
            for c in copies:
                c.wait()
        for j in range(slots):
            slot = (me ^ x) * slots + j
            for i in range(heads):
                to = pl.ds(pl.multiple_of(slot * dim, dim), dim)
                buf[i, to, :] = ins[x][j, i * dim : (i + 1) * dim, :]
            at = pl.multiple_of(slot * EXTRA, EXTRA)
            vectors[pl.ds(at, EXTRA), :] = ins[x][j, depth:, :].astype(F32)
    for x in range(n):
        for j in range(slots):
            middle = parents[1, (me ^ x) * slots + j]
            root = pl.ds(pl.multiple_of(parents[0, middle] * dim, dim), dim)
            for i in range(heads):
                outs[x][j * depth + i * dim : j * depth + (i + 1) * dim, :] = buf[i, root, :]
            for i in range(heads):
                for place, array in enumerate((K, V)):
                    to = j * KEPT + i * 2 + place
                    kept[to : to + 1, :] = vectors[pl.ds(parents[STEPS + 1, (me ^ x) * slots + j] + row_of(i, array, 0), 1), :]
        outs[x][slots * depth : slots * (depth + KEPT), :] = kept[...].astype(BF16)
    line = lax.broadcasted_iota(jnp.int32, (STEPS * total, dim), 0)
    mid_line = lax.broadcasted_iota(jnp.int32, (total, total), 0)
    source = jnp.zeros((STEPS * total, dim), jnp.int32)
    chosen = jnp.zeros((total, total), jnp.int32)
    for c in range(total):
        middle = parents[1, c]
        source = jnp.where(line == c, parents[0, c], source)
        source = jnp.where(line == total + c, parents[0, middle], source)
        chosen = jnp.where(mid_line == c, middle, chosen)
    pick = (chosen == lax.broadcasted_iota(jnp.int32, (total, total), 1)).astype(BF16)
    for i in range(heads):
        d = decay[pl.ds(me * heads + i, 1), :]

        def get(array, step):
            return vectors[pl.ds(row_of(i, array, step), total, stride=EXTRA), :]

        q1, q2, k1, k2 = get(Q, 0), get(Q, 1), get(K, 0), get(K, 1)
        v1, v2 = get(V, 0), get(V, 1)
        queries = jnp.concatenate([q1, q2], 0)
        mine = [jnp.where(source == slot, queries, 0.0).astype(BF16) for slot in range(total)]
        acc = jnp.dot(jnp.concatenate(mine, 1), buf[i], preferred_element_type=F32)
        k1m = jnp.dot(pick, k1.astype(BF16), preferred_element_type=F32)
        v1m = jnp.dot(pick, v1.astype(BF16), preferred_element_type=F32)
        r1 = d * acc[:total] + jnp.sum(q1 * k1, -1, keepdims=True) * v1
        r2 = d * (d * acc[total:] + jnp.sum(q2 * k1m, -1, keepdims=True) * v1m)
        r2 = r2 + jnp.sum(q2 * k2, -1, keepdims=True) * v2
        attn = [jax.nn.sigmoid(get(G, 0)) * r1, jax.nn.sigmoid(get(G, 1)) * r2]
        attn = jnp.concatenate(attn, 0).astype(BF16)
        lines = slice(i * STEPS * total, (i + 1) * STEPS * total)
        attn_out[lines, :] = attn
        outs[n // 2][slots * (depth + KEPT) + lines.start : slots * (depth + KEPT) + lines.stop, :] = attn


def project(n, lines, weight, pieces):
    me = lax.axis_index("beam")
    dim = next(iter(pieces.values()))[0].shape[1]
    heads = weight.shape[0] // dim // n
    acc = None
    for x, (ref, first) in pieces.items():
        rows = pl.ds(pl.multiple_of((me ^ x) * heads * dim, dim), heads * dim)
        lhs = [ref[first + i * lines : first + (i + 1) * lines, :] for i in range(heads)]
        term = jnp.dot(jnp.concatenate(lhs, 1), weight[rows, :], preferred_element_type=F32)
        acc = term if acc is None else acc + term
    return acc


def relay_kernel(have, got, out):
    more = out.shape[0] - have.shape[0]
    out[: have.shape[0], :] = have[...]
    out[have.shape[0] :, :] = got[got.shape[0] - more :, :]


def project_kernel(n, order, head_count, weight, begun, *rest):
    keep, send, terms = rest[-3:]
    pieces = {}
    for places, ref in zip(order, rest):
        pieces |= {x: (ref, at * (ref.shape[0] // len(places))) for at, x in enumerate(places)}
    head, lines = lax.axis_index("head"), terms.shape[0]
    terms[...] = begun[...] + project(n, lines, weight, pieces)
    part = lines // STEPS // head_count
    for t in range(STEPS):
        own = pl.multiple_of(t * part * head_count + head * part, part)
        other = pl.multiple_of(t * part * head_count + (1 - head) * part, part)
        keep[t] = terms[pl.ds(own, part), :]
        send[t] = terms[pl.ds(other, part), :]


def final_kernel(n, order, first, decay, k, v, *rest):
    if first:
        weight, attn, *rest = rest
    ins, (result, *more, out, ks, vs, total, sem) = dict(zip(order, rest)), rest[-7:]
    if first:
        terms = more
    else:
        keep, other = rest[len(order) + 1 : len(order) + 3]
        total[...] = (keep[...] + other[...]).astype(BF16)
        projected = pltpu.make_async_copy(total, more[0], sem.at[n])
        projected.start()
    slots, dim, columns = result.shape
    if first:
        across = ins[n // 2]
        pieces = {0: (attn, 0), n // 2: (across, across.shape[0] - attn.shape[0])}
        terms[0][...] = project(n, terms[0].shape[0], weight, pieces)
    heads = columns // dim // n
    depth = heads * dim
    me = lax.axis_index("beam")
    ks[...] = k[1].astype(F32)
    vs[...] = v[1].astype(F32)
    line = lax.broadcasted_iota(jnp.int32, (16, dim), 0)
    copies = []
    for x in order:
        extra = ins[x][slots * depth : slots * (depth + KEPT), :].astype(F32)
        for j in range(slots):
            for i in range(heads):
                h = (me ^ x) * heads + i
                d = decay[pl.ds(h, 1), :]
                at = pl.ds(pl.multiple_of(h * dim, dim), dim)
                row = j * KEPT + i * 2
                k1, v1 = extra[row : row + 1], extra[row + 1 : row + 2]
                scaled = d * v1
                high = scaled.astype(BF16).astype(F32)
                low = scaled - high
                lhs = jnp.where(line < 2, k1, jnp.where(line == 2, ks[j : j + 1, at], 0.0))
                rhs = jnp.where(line == 0, high, jnp.where(line == 1, low, vs[j : j + 1, at]))
                outer = lax.dot_general(
                    lhs.astype(BF16), rhs.astype(BF16), (((0,), (0,)), ((), ())), preferred_element_type=F32
                )
                begin = j * depth + i * dim
                out[j, :, at] = (d * d) * ins[x][begin : begin + dim, :].astype(F32) + outer
        at = pl.ds(pl.multiple_of((me ^ x) * depth, depth), depth)
        copies.append(pltpu.make_async_copy(out.at[:, :, at], result.at[:, :, at], sem.at[x]))
        copies[-1].start()
    for c in copies:
        c.wait()
    if not first:
        projected.wait()


def fast(n, head_count, states, decay_rates, queries, key_vectors, values, gate_logits, parents, out_weight):
    slots, dim, columns = states.shape
    heads = columns // dim // n
    total, depth = n * slots, heads * dim
    first, second = [4, 1, 2, 3, 5, 6, 7, 0], [4, 1, 2, 3, 5, 6, 7, 0]
    decay = jnp.broadcast_to(jnp.exp(-decay_rates)[:, None], (columns // dim, dim))

    def exchange(order, chunks):
        return [
            lax.ppermute(chunk, "beam", [(j, j ^ x) for j in range(n)]) if x else chunk
            for x, chunk in zip(order, chunks)
        ]

    table = jnp.concatenate([parents, parents * EXTRA], 0)
    packed = []
    for part in (first[:1], first[1:]):
        packed += pl.pallas_call(
            functools.partial(pack_kernel, n, part),
            out_shape=[jax.ShapeDtypeStruct((slots, depth + EXTRA, dim), BF16)] * len(part),
            in_specs=[ANY] * 5,
            out_specs=[ANY] * len(part),
            scratch_shapes=[
                pltpu.VMEM((slots, dim, columns), F32),
                pltpu.VMEM((ARRAYS, *queries.shape), BF16),
                pltpu.VMEM((slots, ARRAYS * STEPS, columns), F32),
                pltpu.VMEM((n, slots, depth + EXTRA, dim), BF16),
                pltpu.SemaphoreType.DMA((n,)),
                pltpu.SemaphoreType.DMA((ARRAYS,)),
                pltpu.SemaphoreType.DMA((n,)),
            ],
        )(states, queries, key_vectors, values, gate_logits)
    packed[-1] = pl.pallas_call(
        hold_kernel,
        out_shape=jax.ShapeDtypeStruct(packed[-1].shape, BF16),
        in_specs=[VMEM],
        out_specs=VMEM,
        compiler_params=params(),
    )(packed[-1])
    attn_shape = jax.ShapeDtypeStruct((heads * STEPS * total, dim), BF16)
    lines = slots * (depth + KEPT)
    *picked, attn = pl.pallas_call(
        functools.partial(middle_kernel, n, first, second),
        out_shape=[
            jax.ShapeDtypeStruct((lines + (attn_shape.shape[0] if x == n // 2 else 0), dim), BF16) for x in second
        ]
        + [attn_shape],
        in_specs=[ANY] + [VMEM] * n + [ANY],
        out_specs=[VMEM] * (n + 1),
        scratch_shapes=[
            pltpu.VMEM((heads, total * dim, dim), BF16),
            pltpu.VMEM(((total + 1) * EXTRA, dim), F32),
            pltpu.VMEM((slots * KEPT, dim), F32),
            pltpu.SMEM(table.shape, jnp.int32),
            pltpu.VMEM((slots, depth + EXTRA, dim), BF16),
            pltpu.SemaphoreType.DMA((2,)),
        ],
        compiler_params=params(),
    )(table, decay, *exchange(first, packed))
    forked = exchange(second, picked)
    held = dict(zip(second, forked))
    have, got, places, hop = attn, held[n // 2], [0, n // 2], 1
    relayed = {}
    while hop < n // 2:
        have = pl.pallas_call(
            relay_kernel,
            out_shape=jax.ShapeDtypeStruct((len(places) * attn.shape[0], dim), BF16),
            in_specs=[VMEM] * 2,
            out_specs=VMEM,
            compiler_params=params(),
        )(have, got)
        (got,) = exchange([hop], [have])
        relayed[tuple(x ^ hop for x in places)] = got
        places += [x ^ hop for x in places]
        hop *= 2

    whole = jax.ShapeDtypeStruct(states.shape, F32)
    summed = jax.ShapeDtypeStruct((STEPS, total // head_count, out_weight.shape[1]), BF16)

    def finish(part, *before):
        more = [] if before else [out_weight, attn]
        return pl.pallas_call(
            functools.partial(final_kernel, n, part, not before),
            out_shape=[whole, summed if before else jax.ShapeDtypeStruct((STEPS * total, out_weight.shape[1]), F32)],
            in_specs=[VMEM] * (len(more) + len(part) + 3) + ([ANY, VMEM, VMEM] if before else []),
            out_specs=[ANY, ANY if before else VMEM],
            input_output_aliases={len(part) + 3: 0} if before else {},
            scratch_shapes=[
                pltpu.VMEM(states.shape, F32),
                pltpu.VMEM((slots, columns), F32),
                pltpu.VMEM((slots, columns), F32),
                pltpu.VMEM(summed.shape, BF16),
                pltpu.SemaphoreType.DMA((n + 1,)),
            ],
            compiler_params=params(),
        )(decay, key_vectors, values, *more, *[held[x] for x in part], *before)

    begun, partial = finish(second[:5] + second[-1:])
    piece = jax.ShapeDtypeStruct((STEPS, total // head_count, out_weight.shape[1]), F32)
    keep, send = pl.pallas_call(
        functools.partial(project_kernel, n, list(relayed), head_count),
        out_shape=[piece, piece],
        in_specs=[VMEM] * (2 + len(relayed)),
        out_specs=[VMEM] * 2,
        scratch_shapes=[pltpu.VMEM((STEPS * total, out_weight.shape[1]), F32)],
        compiler_params=params(),
    )(out_weight, partial, *relayed.values())
    other = lax.ppermute(send, "head", [(0, 1), (1, 0)])
    final, projected = finish(second[5:-1], begun, keep, other)
    return projected, final


def fork(state, parent_list):
    row_state = lax.all_to_all(state, "beam", split_axis=1, concat_axis=0, tiled=True)
    picked = jnp.take(row_state, parent_list, axis=0)
    return lax.all_to_all(picked, "beam", split_axis=0, concat_axis=1, tiled=True)


def general(states, decay_rates, queries, key_vectors, values, gate_logits, parents, out_weight):
    slot_count, head_dim, columns = states.shape
    groups = columns // head_dim
    decay = jnp.exp(-decay_rates)
    current = states
    readouts = []
    for step in range(parents.shape[0]):
        forked = fork(current, parents[step])
        query_f = queries[step].astype(F32).reshape(slot_count, groups, head_dim)
        key_f = key_vectors[step].astype(F32).reshape(slot_count, groups, head_dim)
        value_f = values[step].astype(F32).reshape(slot_count, groups, head_dim)
        grid = forked.reshape(slot_count, head_dim, groups, head_dim)
        updated = decay[None, None, :, None] * grid + jnp.einsum("shi,shj->sihj", key_f, value_f)
        readout = jnp.einsum("shi,sihj->shj", query_f, updated, precision=lax.Precision.HIGHEST)
        current = updated.reshape(slot_count, head_dim, columns)
        readouts.append(readout.reshape(slot_count, columns))
    stacked = jnp.stack(readouts)
    attn = (jax.nn.sigmoid(gate_logits.astype(F32)) * stacked).astype(BF16)
    terms = jnp.einsum(
        "tsc,cd->tsd",
        lax.all_gather(attn, "beam", axis=1, tiled=True),
        out_weight,
        preferred_element_type=F32,
    )
    projected = lax.psum_scatter(terms, "head", scatter_dimension=1, tiled=True).astype(BF16)
    return (projected, current)


def solution(mesh):
    n, head_count = mesh.shape["beam"], mesh.shape["head"]

    def shards(*args):
        columns, dim = args[0].shape[2], args[0].shape[1]
        if n & (n - 1) == 0 and columns // dim == 2 * n and head_count == 2:
            return fast(n, head_count, *args)
        return general(*args)

    in_specs = (
        P(("parts", "beam"), None, "head"),
        P("head"),
        P(None, ("parts", "beam"), "head"),
        P(None, ("parts", "beam"), "head"),
        P(None, ("parts", "beam"), "head"),
        P(None, ("parts", "beam"), "head"),
        P(None, "parts"),
        P("head", "beam"),
    )
    out_specs = (P(None, ("parts", "head"), "beam"), P(("parts", "beam"), None, "head"))
    return jax.shard_map(shards, mesh=mesh, in_specs=in_specs, out_specs=out_specs, check_vma=False)
```
